32 devices in a mesh: gx: 8 (over z, x), gy: 4 (over y, core).
Axes of the slice: x: 2, y: 2, z: 4, core: 2. Of those that a mesh axis runs over, the one named last changes fastest.
Arguments:
- e_field: float32 [3, 128, 128, 128], P(None, 'gx', 'gy'), may hold values from -6 to 6
- h_field: float32 [3, 128, 128, 128], P(None, 'gx', 'gy'), may hold values from -6 to 6
- lorentz_current: float32 [3, 128, 128, 128], P(None, 'gx', 'gy'), may hold values from -3 to 3
- polarization: float32 [3, 128, 128, 128], P(None, 'gx', 'gy'), may hold values from -3 to 3
- material_ids: int32 [128, 128, 128], P('gx', 'gy'), may hold values from 0 to 7
- inv_permittivity: float32 [8], replicated, may hold values from 0.3 to 1
- current_decay: float32 [8], replicated, may hold values from 0.4 to 0.95
- current_drive: float32 [8], replicated, may hold values from 0.3 to 1
- current_restore: float32 [8], replicated, may hold values from 0.2 to 1
- incident_line: float32 [2, 512], P(None, 'gy'), may hold values from -6 to 6
- boundary_mask: int32 [8, 4], replicated, may hold values 0 or 1
- surface_slots: int32 [8, 4, 128], P('gx', 'gy'), may hold values from -1 to 511, as said below
- block_owner: int32 [64], replicated, may hold values from 0 to 31, as said below
Outputs:
- e_out: float32 [3, 128, 128, 128], P(None, 'gx', 'gy')
- h_out: float32 [3, 128, 128, 128], P(None, 'gx', 'gy')
- j_out: float32 [3, 128, 128, 128], P(None, 'gx', 'gy')
- p_out: float32 [3, 128, 128, 128], P(None, 'gx', 'gy')
- far_field: float32 [128, 512], P(('gx', 'gy'))
The draws below stay inside these ranges and needn't reach their ends.
Inputs may be any that keep to these rules, and one draw needn't show every extreme that they name: `block_owner`: each device number names at most 4 blocks, and some device names exactly 4. `surface_slots`: each tile lists distinct surface cells (x within the tile times 32 plus y within the tile) in its first slots and -1 in the rest; at least 32 slots are used on every tile, and some tile uses all 128.
All inputs are finite; a program needn't handle non-finite values.
Results may differ from the reference program's by a relative error of at most 0.0003.
Values sent between devices are 32-bit elements; how exact they have to be, the bound alone decides.
A program may use at most 64 MiB of HBM per device.

```python
import math
import jax
import jax.numpy as jnp
from jax import lax

CX = 16
CY = 32
NZ = 128
STEPS = 4
NMAT = 8
NF = 2
DB = 32
BLK_DEV = 2
SLOTS = 128
NX = 128
NY = 128
BMAX = 4
NBLK = 64
NAUX = 512
Z0 = 32
ZS = 29
N_GX = 8
N_GY = 4


def draw_block_owner(key, part):
    device_count = N_GX * N_GY
    half_count = device_count // 2
    key_a, key_b, key_c = jax.random.split(jax.random.fold_in(key, 11), 3)
    shuffled = jax.random.permutation(key_a, device_count)
    shifted = jax.random.randint(key_b, (half_count,), 0, BLK_DEV + 1)
    shifted = shifted.at[0].set(BLK_DEV)
    counts = jnp.zeros((device_count,), jnp.int32)
    counts = counts.at[shuffled[0::2]].set(BLK_DEV + shifted)
    counts = counts.at[shuffled[1::2]].set(BLK_DEV - shifted)
    owners = jnp.repeat(jnp.arange(device_count, dtype=jnp.int32), counts, total_repeat_length=NBLK)
    return jax.random.permutation(key_c, owners).astype(jnp.int32)


def draw_surface_slots(key, part):
    tile_count = N_GX * N_GY
    cell_count = CX * CY
    key_a, key_b, key_c = jax.random.split(jax.random.fold_in(key, 23), 3)
    counts = jax.random.randint(key_a, (tile_count,), SLOTS // 4, SLOTS + 1)
    full_tile = jax.random.randint(key_b, (), 0, tile_count)
    counts = jnp.where(jnp.arange(tile_count) == full_tile, SLOTS, counts)
    key_list = jax.random.split(key_c, tile_count)
    picked = jax.vmap(lambda one_key: jax.random.permutation(one_key, cell_count)[:SLOTS])(key_list)
    slot_ids = jnp.where(jnp.arange(SLOTS)[None, :] < counts[:, None], picked, -1)
    return slot_ids.reshape(N_GX, N_GY, SLOTS).astype(jnp.int32)


def touch_ends(values, rng, smallest, largest):
    longest = values.shape.index(max(values.shape))
    spots = []
    for shift in (0, 1):
        where = [jax.random.randint(jax.random.fold_in(rng, axis), (), 0, length) for axis, length in enumerate(values.shape)]
        where[longest] = (where[longest] + shift) % values.shape[longest]
        spots.append(tuple(where))
    return values.at[spots[0]].set(smallest).at[spots[1]].set(largest)


def steps_of(rng, shape, pieces, smallest, high):
    factor_of = 1.0
    for dim, parts in pieces:
        steps = jax.random.uniform(jax.random.fold_in(jax.random.fold_in(rng, 6), dim), (parts,), jnp.float32, smallest / len(pieces), high / len(pieces))
        factor_of = factor_of * jnp.repeat(jnp.exp(steps), shape[dim] // parts).reshape((-1,) + (1,) * (len(shape) - 1 - dim))
    return factor_of


def bell_draw(key, extent, width, reach, pieces=(), kind=jnp.bfloat16):
    gain = steps_of(key, extent, pieces, -0.22, 0.18) if pieces else 1.0
    result = jax.random.normal(key, extent, jnp.float32) * width * gain
    return jnp.minimum(jnp.maximum(result, -reach), reach).astype(kind)


def setup_inputs(seed: int = 0) -> dict:
    key_of = jax.random.split(jax.random.key(seed), 14)
    return {
        "e_field": bell_draw(key_of[0], (3, NX, NY, NZ), 1.0, 6.0, ((1, 8), (2, 4)), jnp.float32),
        "h_field": bell_draw(key_of[1], (3, NX, NY, NZ), 1.0, 6.0, ((1, 8), (2, 4)), jnp.float32),
        "lorentz_current": bell_draw(key_of[2], (3, NX, NY, NZ), 0.5, 3.0, ((1, 8), (2, 4)), jnp.float32),
        "polarization": bell_draw(key_of[3], (3, NX, NY, NZ), 0.5, 3.0, ((1, 8), (2, 4)), jnp.float32),
        "material_ids": touch_ends(jax.random.randint(key_of[4], (NX, NY, NZ), 0, NMAT), jax.random.fold_in(key_of[4], 1), 0, NMAT - 1).astype(jnp.int32),
        "inv_permittivity": jnp.clip(jnp.exp(jax.random.uniform(key_of[5], (NMAT,), jnp.float32, math.log(0.3), math.log(1.0))), 0.3, 1.0),
        "current_decay": jnp.clip(jnp.exp(jax.random.uniform(key_of[6], (NMAT,), jnp.float32, math.log(0.4), math.log(0.95))), 0.4, 0.95),
        "current_drive": jnp.clip(jax.random.uniform(key_of[7], (NMAT,), jnp.float32, 0.3, 1.0), 0.3, 1.0),
        "current_restore": jnp.clip(jnp.exp(jax.random.uniform(key_of[8], (NMAT,), jnp.float32, math.log(0.2), math.log(1.0))), 0.2, 1.0),
        "incident_line": bell_draw(key_of[9], (2, NAUX), 1.0, 6.0, ((1, 4),), jnp.float32),
        "boundary_mask": touch_ends((jax.random.randint(key_of[10], (N_GX, N_GY), 0, 2) < 1).astype(jnp.int32), jax.random.fold_in(key_of[10], 1), 0, 1),
        "surface_slots": draw_surface_slots(jax.random.fold_in(key_of[13], 71), 0),
        "block_owner": draw_block_owner(jax.random.fold_in(key_of[13], 71), 0),
    }


FREQS = (0.35, 0.6)
WAVENUMS = (0.7, 1.2)
COURANT = 0.5
HIGHEST = lax.Precision.HIGHEST

def forward_diff(values, which_axis):
    length = values.shape[which_axis]
    upper_part = lax.slice_in_dim(values, 1, length, axis=which_axis)
    widths = [(0, 0)] * values.ndim
    widths[which_axis] = (0, 1)
    return jnp.pad(upper_part, widths) - values

def backward_diff(values, which_axis):
    length = values.shape[which_axis]
    lower_part = lax.slice_in_dim(values, 0, length - 1, axis=which_axis)
    widths = [(0, 0)] * values.ndim
    widths[which_axis] = (1, 0)
    return values - jnp.pad(lower_part, widths)

def advance_magnetic(e_line, h_line):
    e_ahead = jnp.concatenate([e_line[1:], jnp.zeros((1,), e_line.dtype)])
    return h_line - COURANT * (e_ahead - e_line)

def advance_electric(e_line, h_line):
    h_behind = jnp.concatenate([jnp.zeros((1,), h_line.dtype), h_line[:-1]])
    return e_line - COURANT * (h_line - h_behind)

def directions(dir_index, total_dirs):
    along_u = ((dir_index % 64).astype(jnp.float32) + 0.5) / 32.0 - 1.0
    along_v = ((dir_index // 64).astype(jnp.float32) + 0.5) * (128.0 / total_dirs) - 1.0
    return (along_u, along_v)

def radiate(slot_rows, coords_x, coords_y, along_u, along_v):
    spread = along_u[:, None] * coords_x[None, :] + along_v[:, None] * coords_y[None, :]
    pieces_out = []
    for freq_index in range(len(WAVENUMS)):
        phases = WAVENUMS[freq_index] * spread
        cosine = jnp.cos(phases)
        sine_part = jnp.sin(phases)
        real_rows = slot_rows[freq_index * 8:freq_index * 8 + 8:2]
        imag_rows = slot_rows[freq_index * 8 + 1:freq_index * 8 + 8:2]
        real_out = jnp.dot(real_rows, cosine.T, precision=HIGHEST) - jnp.dot(imag_rows, sine_part.T, precision=HIGHEST)
        imag_out = jnp.dot(imag_rows, cosine.T, precision=HIGHEST) + jnp.dot(real_rows, sine_part.T, precision=HIGHEST)
        pieces_out.append(jnp.stack([real_out, imag_out], axis=1).reshape(8, -1))
    return jnp.concatenate(pieces_out, axis=0)

def slot_table(block_owner, per_device):
    count_blocks = block_owner.shape[0]
    order_ids = jnp.arange(count_blocks, dtype=jnp.int32)
    earlier = (order_ids[None, :] < order_ids[:, None]) & (block_owner[None, :] == block_owner[:, None])
    rank_in = lax.optimization_barrier(jnp.sum(earlier.astype(jnp.int32), axis=1))
    return block_owner * per_device + rank_in

def reference(e_field, h_field, lorentz_current, polarization, material_ids, inv_permittivity, current_decay, current_drive, current_restore, incident_line, boundary_mask, surface_slots, block_owner):
    inv_eps = inv_permittivity[material_ids]
    decay_cell = current_decay[material_ids]
    drive_cell = current_drive[material_ids]
    restore_cell = current_restore[material_ids]
    cell_mask = jnp.repeat(jnp.repeat(boundary_mask, CX, axis=0), CY, axis=1).astype(jnp.float32)
    xs_global = jnp.arange(NX, dtype=jnp.int32)
    ys_global = jnp.arange(NY, dtype=jnp.int32)
    inject_index = 2 * (xs_global[:, None] + ys_global[None, :]) + 1
    depth_index = jnp.arange(NZ, dtype=jnp.int32)
    plane_h = depth_index == Z0 - 1
    plane_e = depth_index == Z0
    e_line = incident_line[0]
    h_line = incident_line[1]
    e_now, h_now, j_now, p_now = (e_field, h_field, lorentz_current, polarization)
    currents = jnp.zeros((NF, 4, 2, NX, NY), jnp.float32)
    for step_index in range(STEPS):
        inject_e = e_line[inject_index] * cell_mask
        h_x = h_now[0] - COURANT * (forward_diff(e_now[2], 1) - forward_diff(e_now[1], 2))
        h_y = h_now[1] - COURANT * (forward_diff(e_now[0], 2) - forward_diff(e_now[2], 0)) + COURANT * jnp.where(plane_h, inject_e[:, :, None], 0.0)
        h_z = h_now[2] - COURANT * (forward_diff(e_now[1], 0) - forward_diff(e_now[0], 1))
        h_line = advance_magnetic(e_line, h_line)
        inject_h = h_line[inject_index] * cell_mask
        curl_x = backward_diff(h_z, 1) - backward_diff(h_y, 2) + jnp.where(plane_e, inject_h[:, :, None], 0.0)
        curl_y = backward_diff(h_x, 2) - backward_diff(h_z, 0)
        curl_z = backward_diff(h_y, 0) - backward_diff(h_x, 1)
        curl_all = jnp.stack([curl_x, curl_y, curl_z])
        e_new = e_now + inv_eps[None] * (COURANT * curl_all - j_now)
        j_new = decay_cell[None] * j_now + drive_cell[None] * e_new - restore_cell[None] * p_now
        p_new = p_now + j_new
        e_line = advance_electric(e_line, h_line)
        tangential = jnp.stack([e_new[0, :, :, ZS], e_new[1, :, :, ZS], h_x[:, :, ZS], h_y[:, :, ZS]])
        time_index = step_index + 1
        for freq_index in range(NF):
            weight_cos = math.cos(FREQS[freq_index] * time_index)
            weight_sin = math.sin(FREQS[freq_index] * time_index)
            currents = currents.at[freq_index, :, 0].add(weight_cos * tangential)
            currents = currents.at[freq_index, :, 1].add(-weight_sin * tangential)
        e_now = e_new
        h_now = jnp.stack([h_x, h_y, h_z])
        j_now = j_new
        p_now = p_new
    tile_count = N_GX * N_GY
    flat_slots = surface_slots.reshape(-1)
    slot_valid = (flat_slots >= 0).astype(jnp.float32)
    slot_local = jnp.maximum(flat_slots, 0)
    tile_of = jnp.repeat(jnp.arange(tile_count, dtype=jnp.int32), SLOTS)
    cell_x = tile_of // N_GY * CX + slot_local // CY
    cell_y = tile_of % N_GY * CY + slot_local % CY
    slot_rows = currents.reshape(8 * NF, NX, NY)[:, cell_x, cell_y] * slot_valid[None, :]
    coords_x = cell_x.astype(jnp.float32)
    coords_y = cell_y.astype(jnp.float32)
    total_dirs = NBLK * DB
    dir_span = 256

    def one_block(first_dir):
        along_u, along_v = directions(first_dir + jnp.arange(dir_span, dtype=jnp.int32), total_dirs)
        return radiate(slot_rows, coords_x, coords_y, along_u, along_v)
    firsts = jnp.arange(total_dirs // dir_span, dtype=jnp.int32) * dir_span
    blocks = lax.map(one_block, firsts)
    spectrum = jnp.transpose(blocks, (1, 0, 2)).reshape(8 * NF, NBLK, DB)
    spectrum = jnp.transpose(spectrum, (1, 0, 2)).reshape(NBLK, 8 * NF * DB)
    slot_of = slot_table(block_owner, BMAX)
    onehot = (slot_of[None, :] == jnp.arange(tile_count * BMAX, dtype=jnp.int32)[:, None]).astype(jnp.float32)
    far_scale = 1.0 / math.sqrt(tile_count * SLOTS)
    far_field = jnp.dot(onehot, spectrum, precision=HIGHEST) * far_scale
    return (e_now, h_now, j_now, p_now, far_field)
```

```python
import functools
import math

import jax
import jax.numpy as jnp
import numpy as np
from jax import lax
from jax.experimental import pallas as pl
from jax.experimental.pallas import tpu as pltpu
from jax.sharding import PartitionSpec as P

STEPS = 4
NF = 2
DB = 32
BMAX = 4
FREQS = (0.35, 0.6)
WAVENUMS = (0.7, 1.2)
COURANT = 0.5
HIGHEST = lax.Precision.HIGHEST
MESH = pl.DeviceIdType.MESH
PAD = 8


def phase_tables(gx_n, gy_n, cx, cy, total_dirs):
    nu = 64
    nv = total_dirs // nu
    u = (np.arange(nu) + 0.5) / 32.0 - 1.0
    v = (np.arange(nv) + 0.5) * (128.0 / total_dirs) - 1.0
    ys = np.arange(gy_n * cy).reshape(gy_n, cy)
    xs = np.arange(gx_n * cx)
    vt = np.zeros((gy_n, NF, 2 * nv, cy), np.float32)
    wt = np.zeros((NF, gx_n * cx, 2 * nu), np.float32)
    for f, k in enumerate(WAVENUMS):
        ph = k * v[None, :, None] * ys[:, None, :]
        vt[:, f, :nv] = np.cos(ph)
        vt[:, f, nv:] = np.sin(ph)
        pu = k * xs[:, None] * u[None, :]
        wt[f, :, :nu] = np.cos(pu)
        wt[f, :, nu:] = np.sin(pu)
    return vt, wt


def kernel_body(
    dims,
    mask_s,
    owner_s,
    ieps_s,
    dec_s,
    drv_s,
    res_s,
    e_in,
    h_in,
    j_in,
    p_in,
    mat_in,
    line_in,
    slots_in,
    vt_in,
    wt_in,
    e_out,
    h_out,
    j_out,
    p_out,
    far_out,
    e, h, j, p, mat, coef, line_b, line_o, slots, vt, wt,
    xm, xp, ym, yp, ca, cb, ys1, ys0, cas, cbs, hys, gxh, gyh,
    col_e, col_h, ssum, tsend, trecv, tsr, msend, mall, far,
    in_sem, out_sem, snd, rcv, gsnd, grcv, lsnd, lrcv, fsnd, frcv,
):
    GX, GY, X, Y, Z, NB = dims
    N = GX * GY
    V = N
    c = COURANT
    gx = lax.axis_index("gx")
    gy = lax.axis_index("gy")
    me = gx * GY + gy

    loads = [
        pltpu.make_async_copy(e_in, e.at[:, pl.ds(0, X)], in_sem.at[0]),
        pltpu.make_async_copy(h_in, h, in_sem.at[1]),
        pltpu.make_async_copy(line_in, line_o, in_sem.at[2]),
        pltpu.make_async_copy(mat_in, mat, in_sem.at[3]),
        pltpu.make_async_copy(j_in, j, in_sem.at[4]),
        pltpu.make_async_copy(p_in, p, in_sem.at[5]),
        pltpu.make_async_copy(slots_in, slots, in_sem.at[6]),
        pltpu.make_async_copy(vt_in.at[gy], vt, in_sem.at[7]),
        pltpu.make_async_copy(wt_in, wt, in_sem.at[8]),
    ]
    for cp in loads:
        cp.start()

    has_xm, has_xp = gx > 0, gx < GX - 1
    has_ym, has_yp = gy > 0, gy < GY - 1

    @pl.when(gx == 0)
    def _():
        xm[...] = jnp.zeros_like(xm)
        gxh[...] = jnp.zeros_like(gxh)

    @pl.when(gx == GX - 1)
    def _():
        xp[...] = jnp.zeros_like(xp)

    @pl.when(gy == 0)
    def _():
        ym[...] = jnp.zeros_like(ym)
        gyh[...] = jnp.zeros_like(gyh)

    @pl.when(gy == GY - 1)
    def _():
        yp[...] = jnp.zeros_like(yp)

    @pl.when((gx == 0) | (gy == GY - 1))
    def _():
        ca[...] = jnp.zeros_like(ca)

    @pl.when((gx == GX - 1) | (gy == 0))
    def _():
        cb[...] = jnp.zeros_like(cb)

    barrier = pltpu.get_barrier_semaphore()

    def greet(i, carry):
        d = lax.rem(me + i, N)
        pl.semaphore_signal(barrier, inc=1, device_id=(d // GY, lax.rem(d, GY)), device_id_type=MESH)
        return carry

    lax.fori_loop(1, N, greet, 0)

    loads[0].wait()
    loads[1].wait()

    def pack(x, carry):
        r = pl.ds(x, 1)
        for k in range(3):
            ys1[k, r, :] = e[k, x, pl.ds(Y - 1, 1), :]
        ys0[0, r, :] = e[0, x, pl.ds(0, 1), :]
        ys0[1, r, :] = e[2, x, pl.ds(0, 1), :]
        hys[0, r, :] = h[0, x, pl.ds(Y - 1, 1), :]
        hys[1, r, :] = h[2, x, pl.ds(Y - 1, 1), :]
        return carry

    lax.fori_loop(0, X, pack, 0)
    cas[...] = e[0, X - 1, pl.ds(0, 1), :]
    cbs[...] = e[1, 0, pl.ds(Y - 1, 1), :]
    loads[2].wait()

    pl.semaphore_wait(barrier, N - 1)

    def remote(src, dst, s, r, dx, dy):
        return pltpu.make_async_remote_copy(
            src_ref=src, dst_ref=dst, send_sem=s, recv_sem=r,
            device_id=(gx + dx, gy + dy), device_id_type=MESH,
        )

    def halo(n):
        def cp(src, dst, k, dx, dy):
            return remote(src, dst, snd.at[n, k], rcv.at[n, k], dx, dy)

        return [
            (has_xp, has_xm, cp(e.at[:, X - 1], xm.at[n], 0, 1, 0)),
            (has_xm, has_xp, cp(e.at[pl.ds(1, 2), 0], xp.at[n], 1, -1, 0)),
            (has_yp, has_ym, cp(ys1, ym.at[n], 2, 0, 1)),
            (has_ym, has_yp, cp(ys0, yp.at[n], 3, 0, -1)),
            (has_xp & has_ym, has_xm & has_yp, cp(cas, ca.at[n], 4, 1, -1)),
            (has_xm & has_yp, has_xp & has_ym, cp(cbs, cb.at[n], 5, -1, 1)),
        ]

    first_h = [
        (has_xp, has_xm, remote(h.at[pl.ds(1, 2), X - 1], gxh, gsnd.at[0], grcv.at[0], 1, 0)),
        (has_yp, has_ym, remote(hys, gyh, gsnd.at[1], grcv.at[1], 0, 1)),
    ]
    line_cp = []
    for q in range(1, GY):
        dst_gy = lax.rem(gy + q, GY)
        line_cp.append(
            pltpu.make_async_remote_copy(
                src_ref=line_o, dst_ref=line_b.at[gy], send_sem=lsnd.at[q],
                recv_sem=lrcv.at[q], device_id=(gx, dst_gy), device_id_type=MESH,
            )
        )

    def start(copies):
        for to, _, cp in copies:
            pl.when(to)(cp.start)

    def finish(copies):
        for to, frm, cp in copies:
            pl.when(frm)(cp.wait_recv)
            pl.when(to)(cp.wait_send)

    halo0 = halo(0)
    start(halo0)
    start(first_h)
    for cp in line_cp:
        cp.start()
    line_b[gy] = line_o[...]

    lane = lax.broadcasted_iota(jnp.int32, (Y, Z), 1)
    row = lax.broadcasted_iota(jnp.int32, (Y, Z), 0)
    lane_x = lax.broadcasted_iota(jnp.int32, (X, Z), 1)
    row_x = lax.broadcasted_iota(jnp.int32, (X, Z), 0)
    z_h = Z // 4 - 1
    z_e = Z // 4
    z_s = Z // 4 - 3

    loads[3].wait()

    def table(x, carry):
        m = mat[x]
        outs = [jnp.full((Y, Z), t[0], jnp.float32) for t in (ieps_s, dec_s, drv_s, res_s)]
        for k in range(1, 8):
            hit = m == k
            outs = [jnp.where(hit, t[k], o) for t, o in zip((ieps_s, dec_s, drv_s, res_s), outs)]
        for k in range(4):
            coef[k, x] = outs[k]
        return carry

    lax.fori_loop(0, X, table, 0)

    loads[6].wait()
    sl = slots[...]
    sl_pos = jnp.maximum(sl, 0)
    sl_x = sl_pos // Y
    sl_y = sl_pos - sl_x * Y
    L = sl.shape[-1]
    one_y = ((lax.broadcasted_iota(jnp.int32, (Y, L), 0) == sl_y) & (sl >= 0)).astype(jnp.bfloat16)
    one_x = (lax.rem(lax.broadcasted_iota(jnp.int32, (128, L), 0), X) == sl_x).astype(jnp.bfloat16)
    cell_mask = lax.dot_general(
        one_y, one_x, (((1,), (1,)), ((), ())), preferred_element_type=jnp.float32
    )

    def mine(b, carry):
        cnt, b0, b1, b2, b3 = carry
        hit = owner_s[b] == me
        b0 = jnp.where(hit & (cnt == 0), b, b0)
        b1 = jnp.where(hit & (cnt == 1), b, b1)
        b2 = jnp.where(hit & (cnt == 2), b, b2)
        b3 = jnp.where(hit & (cnt == 3), b, b3)
        return cnt + hit.astype(jnp.int32), b0, b1, b2, b3

    neg = jnp.int32(-1)
    picks = lax.fori_loop(0, NB, mine, (jnp.int32(0), neg, neg, neg, neg))[1:]

    loads[4].wait()
    loads[5].wait()
    for cp in line_cp:
        cp.wait()

    LL = line_o.shape[1]
    R = col_e.shape[1]
    base = gx * X + gy * Y - PAD
    target = 2 * (base + lax.broadcasted_iota(jnp.int32, (R, LL), 0))
    where_l = lax.broadcasted_iota(jnp.int32, (R, LL), 1)
    acc = [jnp.zeros((R, LL), jnp.float32) for _ in range(4)]
    for q in range(GY):
        for par in range(2):
            hit = target + par == where_l + q * LL
            for k in range(2):
                acc[2 * k + par] += jnp.where(hit, line_b[q, pl.ds(k, 1), :], 0.0)
    cols = [jnp.broadcast_to(jnp.sum(a, axis=1, keepdims=True), (R, Z)) for a in acc]
    ev, od, hv, ho = cols
    t2 = 2 * (base + lax.broadcasted_iota(jnp.int32, (R, Z), 0))
    keep_v = ((t2 >= 0) & (t2 < GY * LL)).astype(jnp.float32)
    for n in range(STEPS):
        col_e[n] = od
        ho = (ho - c * (pltpu.roll(ev, R - 1, 0) - od)) * keep_v
        hv = (hv - c * (od - ev)) * keep_v
        col_h[n] = ho
        ev = (ev - c * (hv - pltpu.roll(ho, 1, 0))) * keep_v
        od = (od - c * (ho - hv)) * keep_v

    m_own = mask_s[gx, gy].astype(jnp.float32)
    m_left = mask_s[jnp.maximum(gx - 1, 0), gy].astype(jnp.float32)
    keep_x = has_xm.astype(jnp.float32)
    keep_y = has_ym.astype(jnp.float32)

    def fz(v, ln):
        return jnp.where(ln == Z - 1, 0.0, pltpu.roll(v, Z - 1, 1)) - v

    def bz(v):
        return v - jnp.where(lane == 0, 0.0, pltpu.roll(v, 1, 1))

    def up_y(v, edge):
        return jnp.where(row == Y - 1, edge, pltpu.roll(v, Y - 1, 0))

    def down_y(v, edge):
        return jnp.where(row == 0, edge, pltpu.roll(v, 1, 0))

    finish(first_h)
    for n in range(STEPS):
        finish(halo0 if n == 0 else pending)
        e[1, X] = xp[n, 0]
        e[2, X] = xp[n, 1]
        ex_m, ey_m, ez_m = xm[n, 0], xm[n, 1], xm[n, 2]
        inj = jnp.where(lane == z_h, (c * m_left) * col_e[n, pl.ds(PAD - 1, Y), :], 0.0)
        gh_y = gxh[0] - c * (fz(ex_m, lane) - (e[2, 0] - ez_m)) + inj
        gh_z = gxh[1] - c * ((e[1, 0] - ey_m) - (up_y(ex_m, ca[n]) - ex_m))
        gh_y = gh_y * keep_x
        gh_z = gh_z * keep_x
        gxh[0] = gh_y
        gxh[1] = gh_z
        ex_m, ey_m, ez_m = ym[n, 0], ym[n, 1], ym[n, 2]
        ey_next = jnp.where(row_x == X - 1, cb[n], pltpu.roll(ey_m, X - 1, 0))
        gyh[0] = (gyh[0] - c * ((ys0[1] - ez_m) - fz(ey_m, lane_x))) * keep_y
        gyh[1] = (gyh[1] - c * ((ey_next - ey_m) - (ys0[0] - ex_m))) * keep_y

        def step(x, carry, n=n):
            hy_m, hz_m, plane = carry
            r = pl.ds(x, 1)
            ex, ey, ez = e[0, x], e[1, x], e[2, x]
            ey_x, ez_x = e[1, x + 1], e[2, x + 1]
            hx = h[0, x] - c * ((up_y(ez, yp[n, 1, r, :]) - ez) - fz(ey, lane))
            inj_e = jnp.where(lane == z_h, (c * m_own) * col_e[n, pl.ds(x + PAD, Y), :], 0.0)
            hy = h[1, x] - c * (fz(ex, lane) - (ez_x - ez)) + inj_e
            hz = h[2, x] - c * ((ey_x - ey) - (up_y(ex, yp[n, 0, r, :]) - ex))
            h[0, x] = hx
            h[1, x] = hy
            h[2, x] = hz
            inj_h = jnp.where(lane == z_e, m_own * col_h[n, pl.ds(x + PAD, Y), :], 0.0)
            cx = (hz - down_y(hz, gyh[1, r, :])) - bz(hy) + inj_h
            cy = bz(hx) - (hz - hz_m)
            cz = (hy - hy_m) - (hx - down_y(hx, gyh[0, r, :]))
            ie, dc, dr, rs = coef[0, x], coef[1, x], coef[2, x], coef[3, x]
            new = []
            for k, (old, curl) in enumerate(((ex, cx), (ey, cy), (ez, cz))):
                jo = j[k, x]
                po = p[k, x]
                en = old + ie * (c * curl - jo)
                jn = dc * jo + dr * en - rs * po
                e[k, x] = en
                j[k, x] = jn
                p[k, x] = po + jn
                new.append(en)
            if n < STEPS - 1:
                for k in range(3):
                    ys1[k, r, :] = new[k][Y - 1 : Y]
                ys0[0, r, :] = new[0][0:1]
                ys0[1, r, :] = new[2][0:1]
            l64 = lax.rem(lane, 4 * X)
            for k, val in enumerate((new[0], new[1], hx, hy)):
                plane = jnp.where(l64 == k * X + x, val[:, z_s : z_s + 1], plane)
            return hy, hz, plane

        zero = jnp.zeros((Y, Z), jnp.float32)
        plane = lax.fori_loop(0, X, step, (gh_y, gh_z, zero))[2]
        if n < STEPS - 1:
            cas[...] = e[0, X - 1, pl.ds(0, 1), :]
            cbs[...] = e[1, 0, pl.ds(Y - 1, 1), :]
            pending = halo(n + 1)
            start(pending)
        for f in range(NF):
            wc = math.cos(FREQS[f] * (n + 1))
            ws = -math.sin(FREQS[f] * (n + 1))
            add = jnp.where(lane < 4 * X, wc, ws) * plane
            ssum[f] = add if n == 0 else ssum[f] + add

    stores = [
        pltpu.make_async_copy(e.at[:, pl.ds(0, X)], e_out, out_sem.at[0]),
        pltpu.make_async_copy(h, h_out, out_sem.at[1]),
        pltpu.make_async_copy(j, j_out, out_sem.at[2]),
        pltpu.make_async_copy(p, p_out, out_sem.at[3]),
    ]
    for cp in stores:
        cp.start()

    loads[7].wait()
    loads[8].wait()
    lane_v = lax.broadcasted_iota(jnp.int32, (V, 128), 1)
    for f in range(NF):
        cd = jnp.dot(vt[f], ssum[f] * cell_mask, precision=HIGHEST, preferred_element_type=jnp.float32)
        turned = pltpu.roll(cd[V:], 64, 1)
        t = cd[:V] + jnp.where(lane_v < 64, -turned, turned)
        for v in range(V):
            tsend[v, pl.ds(f, 1), :] = t[v : v + 1]

    def send_t(i, carry):
        d = lax.rem(me + i, N)
        pltpu.make_async_remote_copy(
            src_ref=tsend.at[d], dst_ref=trecv.at[me], send_sem=fsnd.at[0], recv_sem=frcv.at[0],
            device_id=(d // GY, lax.rem(d, GY)), device_id_type=MESH,
        ).start()
        return carry

    lax.fori_loop(1, N, send_t, 0)
    trecv[me] = tsend[me]
    part = pl.ds(0, N - 1)
    pltpu.make_async_copy(trecv.at[part], trecv.at[part], frcv.at[0]).wait()

    for q in range(GX):
        total = trecv[q * GY]
        for s in range(1, GY):
            total = total + trecv[q * GY + s]
        for f in range(NF):
            tsr[f, pl.ds(q, 1), :] = total[f : f + 1]

    l8 = lax.broadcasted_iota(jnp.int32, (8, 128), 1)
    r8 = lax.broadcasted_iota(jnp.int32, (8, 128), 0)
    blk = l8 // X
    grp = l8 // 32
    rows_out = [None] * 8
    for f in range(NF):
        g = jnp.zeros((8, 128), jnp.float32)
        for o in range(GX // 8):
            a = tsr[f, pl.ds(8 * o, 8), :]
            for s in (4, 2, 1):
                from_down = pltpu.roll(pltpu.roll(a, 8 - s, 0), X * s, 1)
                from_up = pltpu.roll(pltpu.roll(a, s, 0), 128 - X * s, 1)
                bi = (r8 & s) != 0
                bj = (blk & s) != 0
                a = jnp.where(bi == bj, a, jnp.where(bj, from_down, from_up))
            g = g + jnp.dot(a, wt[f, pl.ds(o * 128, 128), :], precision=HIGHEST,
                            preferred_element_type=jnp.float32)
        for hh in range(2):
            rep = []
            for cs in range(2):
                w = jnp.where(grp == cs * 2 + hh, g, 0.0)
                w = w + pltpu.roll(w, 32, 1)
                rep.append(w + pltpu.roll(w, 64, 1))
            for chi in range(2):
                comp = chi * 2 + grp // 2
                part_b = grp & 1
                same = r8 == part_b * 4 + comp
                other = r8 == (1 - part_b) * 4 + comp
                sgn = jnp.where(part_b == 1, 1.0, -1.0)
                mix = jnp.where(same, rep[0], 0.0) + jnp.where(other, sgn * rep[1], 0.0)
                rows_out[hh * 4 + f * 2 + chi] = jnp.sum(mix, axis=0, keepdims=True)
    scale = 1.0 / math.sqrt(N * L)
    for i in range(8):
        msend[pl.ds(i, 1), :] = rows_out[i] * scale

    def send_m(i, carry):
        d = lax.rem(me + i, N)
        pltpu.make_async_remote_copy(
            src_ref=msend, dst_ref=mall.at[me], send_sem=fsnd.at[1], recv_sem=frcv.at[1],
            device_id=(d // GY, lax.rem(d, GY)), device_id_type=MESH,
        ).start()
        return carry

    lax.fori_loop(1, N, send_m, 0)
    mall[me] = msend[...]
    pltpu.make_async_copy(mall.at[part], mall.at[part], frcv.at[1]).wait()
    for r in range(BMAX):
        b = picks[r]
        ok = (b >= 0).astype(jnp.float32)
        bb = jnp.maximum(b, 0)
        tile = mall[bb // 2] * ok
        half = jnp.where(lax.rem(bb, 2) == 1, tile[4:8], tile[0:4])
        for k in range(4):
            far[pl.ds(r, 1), pl.ds(k * 128, 128)] = half[k : k + 1]
    last = pltpu.make_async_copy(far, far_out, out_sem.at[4])
    last.start()
    pltpu.make_async_copy(tsend.at[part], tsend.at[part], fsnd.at[0]).wait()
    pltpu.make_async_copy(mall.at[part], mall.at[part], fsnd.at[1]).wait()
    for cp in stores:
        cp.wait()
    last.wait()


def shards(e, h, jc, pz, mat, ieps, dec, drv, res, line, mask, slots, owner, gx_n=0, gy_n=0):
    _, X, Y, Z = e.shape
    N = gx_n * gy_n
    NB = owner.shape[0]
    vt, wt = phase_tables(gx_n, gy_n, X, Y, NB * DB)
    f32 = jnp.float32
    any_spec = pl.BlockSpec(memory_space=pl.ANY)
    smem = pl.BlockSpec(memory_space=pltpu.SMEM)
    field = jax.ShapeDtypeStruct((3, X, Y, Z), f32)
    rows = X + Y + 2 * PAD
    VM = pltpu.VMEM
    dma = pltpu.SemaphoreType.DMA
    scratch = [
        VM((3, X + 1, Y, Z), f32), VM((3, X, Y, Z), f32), VM((3, X, Y, Z), f32),
        VM((3, X, Y, Z), f32), VM((X, Y, Z), jnp.int32), VM((4, X, Y, Z), f32),
        VM((gy_n,) + line.shape, f32), VM(line.shape, f32), VM((1, slots.shape[-1]), jnp.int32),
        VM(vt.shape[1:], f32), VM(wt.shape, f32),
        VM((STEPS, 3, Y, Z), f32), VM((STEPS, 2, Y, Z), f32), VM((STEPS, 3, X, Z), f32),
        VM((STEPS, 2, X, Z), f32), VM((STEPS, 1, Z), f32), VM((STEPS, 1, Z), f32),
        VM((3, X, Z), f32), VM((2, X, Z), f32), VM((1, Z), f32), VM((1, Z), f32),
        VM((2, X, Z), f32), VM((2, Y, Z), f32), VM((2, X, Z), f32),
        VM((STEPS, rows, Z), f32), VM((STEPS, rows, Z), f32), VM((NF, Y, 128), f32),
        VM((N, NF, 128), f32), VM((N, NF, 128), f32), VM((NF, gx_n, 128), f32),
        VM((8, 128), f32), VM((N, 8, 128), f32), VM((BMAX, 512), f32),
        dma((9,)), dma((5,)), dma((STEPS, 6)), dma((STEPS, 6)), dma((2,)), dma((2,)),
        dma((gy_n,)), dma((gy_n,)), dma((2,)), dma((2,)),
    ]
    return pl.pallas_call(
        functools.partial(kernel_body, (gx_n, gy_n, X, Y, Z, NB)),
        out_shape=(field, field, field, field, jax.ShapeDtypeStruct((BMAX, 16 * DB), f32)),
        in_specs=[smem] * 6 + [any_spec] * 9,
        out_specs=(any_spec,) * 5,
        scratch_shapes=scratch,
        compiler_params=pltpu.CompilerParams(
            collective_id=0, has_side_effects=True, vmem_limit_bytes=40 * 1024 * 1024
        ),
        name="yee",
    )(mask, owner, ieps, dec, drv, res, e, h, jc, pz, mat, line, slots.reshape(1, -1),
      jnp.asarray(vt), jnp.asarray(wt))


def solution(mesh):
    field = P(None, "gx", "gy", None)
    in_specs = (
        field, field, field, field, P("gx", "gy", None), P(), P(), P(), P(),
        P(None, "gy"), P(), P("gx", "gy", None), P(),
    )
    out_specs = (field, field, field, field, P(("gx", "gy"), None))
    body = functools.partial(shards, gx_n=mesh.shape["gx"], gy_n=mesh.shape["gy"])
    return jax.shard_map(body, mesh=mesh, in_specs=in_specs, out_specs=out_specs, check_vma=False)
```

```python
import functools
import math

import jax
import jax.numpy as jnp
import numpy as np
from jax import lax
from jax.experimental import pallas as pl
from jax.experimental.pallas import tpu as pltpu
from jax.sharding import PartitionSpec as P

STEPS = 4
NF = 2
DB = 32
BMAX = 4
FREQS = (0.35, 0.6)
WAVENUMS = (0.7, 1.2)
COURANT = 0.5
HIGHEST = lax.Precision.HIGHEST
MESH = pl.DeviceIdType.MESH
PAD = 8


def phase_tables(gx_n, gy_n, cx, cy, total_dirs):
    nu = 64
    nv = total_dirs // nu
    u = (np.arange(nu) + 0.5) / 32.0 - 1.0
    v = (np.arange(nv) + 0.5) * (128.0 / total_dirs) - 1.0
    ys = np.arange(gy_n * cy).reshape(gy_n, cy)
    xs = np.arange(gx_n * cx)
    vt = np.zeros((gy_n, NF, 2 * nv, cy), np.float32)
    wt = np.zeros((NF, gx_n * cx, 2 * nu), np.float32)
    for f, k in enumerate(WAVENUMS):
        ph = k * v[None, :, None] * ys[:, None, :]
        vt[:, f, :nv] = np.cos(ph)
        vt[:, f, nv:] = np.sin(ph)
        pu = k * xs[:, None] * u[None, :]
        wt[f, :, :nu] = np.cos(pu)
        wt[f, :, nu:] = np.sin(pu)
    return vt, wt


def kernel_body(
    dims,
    mask_s,
    owner_s,
    ieps_s,
    dec_s,
    drv_s,
    res_s,
    e_in,
    h_in,
    j_in,
    p_in,
    mat_in,
    line_in,
    slots_in,
    vt_in,
    wt_in,
    e_out,
    h_out,
    j_out,
    p_out,
    far_out,
    e_a, h_a, j_a, p_a, e_b, h_b, j_b, p_b, mat, coef, line_b, line_o, slots, vt, wt,
    xm, xp, ym, yp, ca, cb, ys1, ys0, cas, cbs, hys, gxh, gyh,
    col_e, col_h, ssum, tsend, trecv, tsr, msend, mall, far,
    in_sem, out_sem, snd, rcv, gsnd, grcv, lsnd, lrcv, fsnd, frcv,
):
    GX, GY, X, Y, Z, NB = dims
    N = GX * GY
    V = N
    c = COURANT
    gx = lax.axis_index("gx")
    gy = lax.axis_index("gy")
    me = gx * GY + gy
    e, h, j, p = e_a, h_a, j_a, p_a
    states = ((e_a, h_a, j_a, p_a), (e_b, h_b, j_b, p_b))

    loads = [
        pltpu.make_async_copy(e_in, e.at[:, pl.ds(0, X)], in_sem.at[0]),
        pltpu.make_async_copy(h_in, h, in_sem.at[1]),
        pltpu.make_async_copy(line_in, line_o, in_sem.at[2]),
        pltpu.make_async_copy(mat_in, mat, in_sem.at[3]),
        pltpu.make_async_copy(j_in, j, in_sem.at[4]),
        pltpu.make_async_copy(p_in, p, in_sem.at[5]),
        pltpu.make_async_copy(slots_in, slots, in_sem.at[6]),
        pltpu.make_async_copy(vt_in.at[gy], vt, in_sem.at[7]),
        pltpu.make_async_copy(wt_in, wt, in_sem.at[8]),
    ]
    for cp in loads:
        cp.start()

    has_xm, has_xp = gx > 0, gx < GX - 1
    has_ym, has_yp = gy > 0, gy < GY - 1

    @pl.when(gx == 0)
    def _():
        xm[...] = jnp.zeros_like(xm)
        gxh[...] = jnp.zeros_like(gxh)

    @pl.when(gx == GX - 1)
    def _():
        xp[...] = jnp.zeros_like(xp)

    @pl.when(gy == 0)
    def _():
        ym[...] = jnp.zeros_like(ym)
        gyh[...] = jnp.zeros_like(gyh)

    @pl.when(gy == GY - 1)
    def _():
        yp[...] = jnp.zeros_like(yp)

    @pl.when((gx == 0) | (gy == GY - 1))
    def _():
        ca[...] = jnp.zeros_like(ca)

    @pl.when((gx == GX - 1) | (gy == 0))
    def _():
        cb[...] = jnp.zeros_like(cb)

    barrier = pltpu.get_barrier_semaphore()

    def greet(i, carry):
        d = lax.rem(me + i, N)
        pl.semaphore_signal(barrier, inc=1, device_id=(d // GY, lax.rem(d, GY)), device_id_type=MESH)
        return carry

    lax.fori_loop(1, N, greet, 0)

    loads[0].wait()
    loads[1].wait()

    def pack(x, carry):
        r = pl.ds(x, 1)
        for k in range(3):
            ys1[k, r, :] = e[k, x, pl.ds(Y - 1, 1), :]
        ys0[0, r, :] = e[0, x, pl.ds(0, 1), :]
        ys0[1, r, :] = e[2, x, pl.ds(0, 1), :]
        hys[0, r, :] = h[0, x, pl.ds(Y - 1, 1), :]
        hys[1, r, :] = h[2, x, pl.ds(Y - 1, 1), :]
        return carry

    lax.fori_loop(0, X, pack, 0)
    cas[...] = e[0, X - 1, pl.ds(0, 1), :]
    cbs[...] = e[1, 0, pl.ds(Y - 1, 1), :]
    loads[2].wait()

    pl.semaphore_wait(barrier, N - 1)

    def remote(src, dst, s, r, dx, dy):
        return pltpu.make_async_remote_copy(
            src_ref=src, dst_ref=dst, send_sem=s, recv_sem=r,
            device_id=(gx + dx, gy + dy), device_id_type=MESH,
        )

    def halo(n):
        def cp(src, dst, k, dx, dy):
            return remote(src, dst, snd.at[n, k], rcv.at[n, k], dx, dy)

        return [
            (has_xp, has_xm, cp(states[n % 2][0].at[:, X - 1], xm.at[n], 0, 1, 0)),
            (has_xm, has_xp, cp(states[n % 2][0].at[pl.ds(1, 2), 0], xp.at[n], 1, -1, 0)),
            (has_yp, has_ym, cp(ys1, ym.at[n], 2, 0, 1)),
            (has_ym, has_yp, cp(ys0, yp.at[n], 3, 0, -1)),
            (has_xp & has_ym, has_xm & has_yp, cp(cas, ca.at[n], 4, 1, -1)),
            (has_xm & has_yp, has_xp & has_ym, cp(cbs, cb.at[n], 5, -1, 1)),
        ]

    first_h = [
        (has_xp, has_xm, remote(h.at[pl.ds(1, 2), X - 1], gxh, gsnd.at[0], grcv.at[0], 1, 0)),
        (has_yp, has_ym, remote(hys, gyh, gsnd.at[1], grcv.at[1], 0, 1)),
    ]
    line_cp = []
    for q in range(1, GY):
        dst_gy = lax.rem(gy + q, GY)
        line_cp.append(
            pltpu.make_async_remote_copy(
                src_ref=line_o, dst_ref=line_b.at[gy], send_sem=lsnd.at[q],
                recv_sem=lrcv.at[q], device_id=(gx, dst_gy), device_id_type=MESH,
            )
        )

    def start(copies):
        for to, _, cp in copies:
            pl.when(to)(cp.start)

    def finish(copies):
        for to, frm, cp in copies:
            pl.when(frm)(cp.wait_recv)
            pl.when(to)(cp.wait_send)

    halo0 = halo(0)
    start(halo0)
    start(first_h)
    for cp in line_cp:
        cp.start()
    line_b[gy] = line_o[...]

    lane = lax.broadcasted_iota(jnp.int32, (Y, Z), 1)
    row = lax.broadcasted_iota(jnp.int32, (Y, Z), 0)
    lane_x = lax.broadcasted_iota(jnp.int32, (X, Z), 1)
    row_x = lax.broadcasted_iota(jnp.int32, (X, Z), 0)
    z_h = Z // 4 - 1
    z_e = Z // 4
    z_s = Z // 4 - 3

    loads[3].wait()

    def table(x, carry):
        m = mat[x]
        outs = [jnp.full((Y, Z), t[0], jnp.float32) for t in (ieps_s, dec_s, drv_s, res_s)]
        for k in range(1, 8):
            hit = m == k
            outs = [jnp.where(hit, t[k], o) for t, o in zip((ieps_s, dec_s, drv_s, res_s), outs)]
        for k in range(4):
            coef[k, x] = outs[k]
        return carry

    lax.fori_loop(0, X, table, 0)

    loads[4].wait()
    loads[5].wait()
    for cp in line_cp:
        cp.wait()

    LL = line_o.shape[1]
    R = col_e.shape[1]
    base = gx * X + gy * Y - PAD
    target = 2 * (base + lax.broadcasted_iota(jnp.int32, (R, LL), 0))
    where_l = lax.broadcasted_iota(jnp.int32, (R, LL), 1)
    acc = [jnp.zeros((R, LL), jnp.float32) for _ in range(4)]
    for q in range(GY):
        for par in range(2):
            hit = target + par == where_l + q * LL
            for k in range(2):
                acc[2 * k + par] += jnp.where(hit, line_b[q, pl.ds(k, 1), :], 0.0)
    cols = [jnp.broadcast_to(jnp.sum(a, axis=1, keepdims=True), (R, Z)) for a in acc]
    ev, od, hv, ho = cols
    t2 = 2 * (base + lax.broadcasted_iota(jnp.int32, (R, Z), 0))
    keep_v = ((t2 >= 0) & (t2 < GY * LL)).astype(jnp.float32)
    for n in range(STEPS):
        col_e[n] = od
        ho = (ho - c * (pltpu.roll(ev, R - 1, 0) - od)) * keep_v
        hv = (hv - c * (od - ev)) * keep_v
        col_h[n] = ho
        ev = (ev - c * (hv - pltpu.roll(ho, 1, 0))) * keep_v
        od = (od - c * (ho - hv)) * keep_v

    m_own = mask_s[gx, gy].astype(jnp.float32)
    m_left = mask_s[jnp.maximum(gx - 1, 0), gy].astype(jnp.float32)
    keep_x = has_xm.astype(jnp.float32)
    keep_y = has_ym.astype(jnp.float32)

    def fz(v, ln):
        return jnp.where(ln == Z - 1, 0.0, pltpu.roll(v, Z - 1, 1)) - v

    def bz(v):
        return v - jnp.where(lane == 0, 0.0, pltpu.roll(v, 1, 1))

    def up_y(v, edge):
        return jnp.where(row == Y - 1, edge, pltpu.roll(v, Y - 1, 0))

    def down_y(v, edge):
        return jnp.where(row == 0, edge, pltpu.roll(v, 1, 0))

    finish(first_h)
    for n in range(STEPS):
        e, h, j, p = states[n % 2]
        e_n, h_n, j_n, p_n = states[(n + 1) % 2]
        finish(halo0 if n == 0 else pending)
        e[1, X] = xp[n, 0]
        e[2, X] = xp[n, 1]
        ex_m, ey_m, ez_m = xm[n, 0], xm[n, 1], xm[n, 2]
        inj = jnp.where(lane == z_h, (c * m_left) * col_e[n, pl.ds(PAD - 1, Y), :], 0.0)
        gh_y = gxh[0] - c * (fz(ex_m, lane) - (e[2, 0] - ez_m)) + inj
        gh_z = gxh[1] - c * ((e[1, 0] - ey_m) - (up_y(ex_m, ca[n]) - ex_m))
        gh_y = gh_y * keep_x
        gh_z = gh_z * keep_x
        gxh[0] = gh_y
        gxh[1] = gh_z
        ex_m, ey_m, ez_m = ym[n, 0], ym[n, 1], ym[n, 2]
        ey_next = jnp.where(row_x == X - 1, cb[n], pltpu.roll(ey_m, X - 1, 0))
        gyh[0] = (gyh[0] - c * ((ys0[1] - ez_m) - fz(ey_m, lane_x))) * keep_y
        gyh[1] = (gyh[1] - c * ((ey_next - ey_m) - (ys0[0] - ex_m))) * keep_y

        def step(x, carry, n=n, e=e, h=h, j=j, p=p, e_n=e_n, h_n=h_n, j_n=j_n, p_n=p_n):
            hy_m, hz_m, plane = carry
            r = pl.ds(x, 1)
            ex, ey, ez = e[0, x], e[1, x], e[2, x]
            ey_x, ez_x = e[1, x + 1], e[2, x + 1]
            hx = h[0, x] - c * ((up_y(ez, yp[n, 1, r, :]) - ez) - fz(ey, lane))
            inj_e = jnp.where(lane == z_h, (c * m_own) * col_e[n, pl.ds(x + PAD, Y), :], 0.0)
            hy = h[1, x] - c * (fz(ex, lane) - (ez_x - ez)) + inj_e
            hz = h[2, x] - c * ((ey_x - ey) - (up_y(ex, yp[n, 0, r, :]) - ex))
            h_n[0, x] = hx
            h_n[1, x] = hy
            h_n[2, x] = hz
            inj_h = jnp.where(lane == z_e, m_own * col_h[n, pl.ds(x + PAD, Y), :], 0.0)
            cx = (hz - down_y(hz, gyh[1, r, :])) - bz(hy) + inj_h
            cy = bz(hx) - (hz - hz_m)
            cz = (hy - hy_m) - (hx - down_y(hx, gyh[0, r, :]))
            ie, dc, dr, rs = coef[0, x], coef[1, x], coef[2, x], coef[3, x]
            new = []
            for k, (old, curl) in enumerate(((ex, cx), (ey, cy), (ez, cz))):
                jo = j[k, x]
                po = p[k, x]
                en = old + ie * (c * curl - jo)
                jn = dc * jo + dr * en - rs * po
                e_n[k, x] = en
                j_n[k, x] = jn
                p_n[k, x] = po + jn
                new.append(en)
            if n < STEPS - 1:
                for k in range(3):
                    ys1[k, r, :] = new[k][Y - 1 : Y]
                ys0[0, r, :] = new[0][0:1]
                ys0[1, r, :] = new[2][0:1]
            l64 = lax.rem(lane, 4 * X)
            for k, val in enumerate((new[0], new[1], hx, hy)):
                plane = jnp.where(l64 == k * X + x, val[:, z_s : z_s + 1], plane)
            return hy, hz, plane

        zero = jnp.zeros((Y, Z), jnp.float32)
        plane = lax.fori_loop(0, X, step, (gh_y, gh_z, zero), unroll=4)[2]
        if n < STEPS - 1:
            cas[...] = e_n[0, X - 1, pl.ds(0, 1), :]
            cbs[...] = e_n[1, 0, pl.ds(Y - 1, 1), :]
            pending = halo(n + 1)
            start(pending)
        if n == 0:
            loads[6].wait()
            sl = slots[...]
            sl_pos = jnp.maximum(sl, 0)
            sl_x = sl_pos // Y
            sl_y = sl_pos - sl_x * Y
            L = sl.shape[-1]
            one_y = ((lax.broadcasted_iota(jnp.int32, (Y, L), 0) == sl_y) & (sl >= 0)).astype(jnp.bfloat16)
            one_x = (lax.rem(lax.broadcasted_iota(jnp.int32, (128, L), 0), X) == sl_x).astype(jnp.bfloat16)
            cell_mask = lax.dot_general(
                one_y, one_x, (((1,), (1,)), ((), ())), preferred_element_type=jnp.float32
            )
        if n == 1:
            def mine(b, carry):
                cnt, b0, b1, b2, b3 = carry
                hit = owner_s[b] == me
                b0 = jnp.where(hit & (cnt == 0), b, b0)
                b1 = jnp.where(hit & (cnt == 1), b, b1)
                b2 = jnp.where(hit & (cnt == 2), b, b2)
                b3 = jnp.where(hit & (cnt == 3), b, b3)
                return cnt + hit.astype(jnp.int32), b0, b1, b2, b3

            neg = jnp.int32(-1)
            picks = lax.fori_loop(0, NB, mine, (jnp.int32(0), neg, neg, neg, neg))[1:]
        for f in range(NF):
            wc = math.cos(FREQS[f] * (n + 1))
            ws = -math.sin(FREQS[f] * (n + 1))
            add = jnp.where(lane < 4 * X, wc, ws) * plane
            ssum[f] = add if n == 0 else ssum[f] + add

    e, h, j, p = states[STEPS % 2]
    stores = [
        pltpu.make_async_copy(e.at[:, pl.ds(0, X)], e_out, out_sem.at[0]),
        pltpu.make_async_copy(h, h_out, out_sem.at[1]),
        pltpu.make_async_copy(j, j_out, out_sem.at[2]),
        pltpu.make_async_copy(p, p_out, out_sem.at[3]),
    ]
    for cp in stores:
        cp.start()

    loads[7].wait()
    loads[8].wait()
    lane_v = lax.broadcasted_iota(jnp.int32, (V, 128), 1)
    for f in range(NF):
        cd = jnp.dot(vt[f], ssum[f] * cell_mask, precision=HIGHEST, preferred_element_type=jnp.float32)
        turned = pltpu.roll(cd[V:], 64, 1)
        t = cd[:V] + jnp.where(lane_v < 64, -turned, turned)
        for v in range(V):
            tsend[v, pl.ds(f, 1), :] = t[v : v + 1]

    def send_t(i, carry):
        d = lax.rem(me + i, N)
        pltpu.make_async_remote_copy(
            src_ref=tsend.at[d], dst_ref=trecv.at[me], send_sem=fsnd.at[0], recv_sem=frcv.at[0],
            device_id=(d // GY, lax.rem(d, GY)), device_id_type=MESH,
        ).start()
        return carry

    lax.fori_loop(1, N, send_t, 0)
    trecv[me] = tsend[me]
    part = pl.ds(0, N - 1)
    pltpu.make_async_copy(trecv.at[part], trecv.at[part], frcv.at[0]).wait()

    for q in range(GX):
        total = trecv[q * GY]
        for s in range(1, GY):
            total = total + trecv[q * GY + s]
        for f in range(NF):
            tsr[f, pl.ds(q, 1), :] = total[f : f + 1]

    l8 = lax.broadcasted_iota(jnp.int32, (8, 128), 1)
    r8 = lax.broadcasted_iota(jnp.int32, (8, 128), 0)
    blk = l8 // X
    grp = l8 // 32
    rows_out = [None] * 8
    for f in range(NF):
        g = jnp.zeros((8, 128), jnp.float32)
        for o in range(GX // 8):
            a = tsr[f, pl.ds(8 * o, 8), :]
            for s in (4, 2, 1):
                from_down = pltpu.roll(pltpu.roll(a, 8 - s, 0), X * s, 1)
                from_up = pltpu.roll(pltpu.roll(a, s, 0), 128 - X * s, 1)
                bi = (r8 & s) != 0
                bj = (blk & s) != 0
                a = jnp.where(bi == bj, a, jnp.where(bj, from_down, from_up))
            g = g + jnp.dot(a, wt[f, pl.ds(o * 128, 128), :], precision=HIGHEST,
                            preferred_element_type=jnp.float32)
        for hh in range(2):
            rep = []
            for cs in range(2):
                w = jnp.where(grp == cs * 2 + hh, g, 0.0)
                w = w + pltpu.roll(w, 32, 1)
                rep.append(w + pltpu.roll(w, 64, 1))
            for chi in range(2):
                comp = chi * 2 + grp // 2
                part_b = grp & 1
                same = r8 == part_b * 4 + comp
                other = r8 == (1 - part_b) * 4 + comp
                sgn = jnp.where(part_b == 1, 1.0, -1.0)
                mix = jnp.where(same, rep[0], 0.0) + jnp.where(other, sgn * rep[1], 0.0)
                rows_out[hh * 4 + f * 2 + chi] = jnp.sum(mix, axis=0, keepdims=True)
    scale = 1.0 / math.sqrt(N * L)
    for i in range(8):
        msend[pl.ds(i, 1), :] = rows_out[i] * scale

    def send_m(i, carry):
        d = lax.rem(me + i, N)
        pltpu.make_async_remote_copy(
            src_ref=msend, dst_ref=mall.at[me], send_sem=fsnd.at[1], recv_sem=frcv.at[1],
            device_id=(d // GY, lax.rem(d, GY)), device_id_type=MESH,
        ).start()
        return carry

    lax.fori_loop(1, N, send_m, 0)
    mall[me] = msend[...]
    pltpu.make_async_copy(mall.at[part], mall.at[part], frcv.at[1]).wait()
    for r in range(BMAX):
        b = picks[r]
        ok = (b >= 0).astype(jnp.float32)
        bb = jnp.maximum(b, 0)
        tile = mall[bb // 2] * ok
        half = jnp.where(lax.rem(bb, 2) == 1, tile[4:8], tile[0:4])
        for k in range(4):
            far[pl.ds(r, 1), pl.ds(k * 128, 128)] = half[k : k + 1]
    last = pltpu.make_async_copy(far, far_out, out_sem.at[4])
    last.start()
    pltpu.make_async_copy(tsend.at[part], tsend.at[part], fsnd.at[0]).wait()
    pltpu.make_async_copy(mall.at[part], mall.at[part], fsnd.at[1]).wait()
    for cp in stores:
        cp.wait()
    last.wait()


def shards(e, h, jc, pz, mat, ieps, dec, drv, res, line, mask, slots, owner, gx_n=0, gy_n=0):
    _, X, Y, Z = e.shape
    N = gx_n * gy_n
    NB = owner.shape[0]
    vt, wt = phase_tables(gx_n, gy_n, X, Y, NB * DB)
    f32 = jnp.float32
    any_spec = pl.BlockSpec(memory_space=pl.ANY)
    hbm = pl.BlockSpec(memory_space=pltpu.HBM)
    smem = pl.BlockSpec(memory_space=pltpu.SMEM)
    field = jax.ShapeDtypeStruct((3, X, Y, Z), f32)
    rows = X + Y + 2 * PAD
    VM = pltpu.VMEM
    dma = pltpu.SemaphoreType.DMA
    scratch = [
        VM((3, X + 1, Y, Z), f32), VM((3, X, Y, Z), f32), VM((3, X, Y, Z), f32),
        VM((3, X, Y, Z), f32), VM((3, X + 1, Y, Z), f32), VM((3, X, Y, Z), f32),
        VM((3, X, Y, Z), f32), VM((3, X, Y, Z), f32), VM((X, Y, Z), jnp.int32), VM((4, X, Y, Z), f32),
        VM((gy_n,) + line.shape, f32), VM(line.shape, f32), VM((1, slots.shape[-1]), jnp.int32),
        VM(vt.shape[1:], f32), VM(wt.shape, f32),
        VM((STEPS, 3, Y, Z), f32), VM((STEPS, 2, Y, Z), f32), VM((STEPS, 3, X, Z), f32),
        VM((STEPS, 2, X, Z), f32), VM((STEPS, 1, Z), f32), VM((STEPS, 1, Z), f32),
        VM((3, X, Z), f32), VM((2, X, Z), f32), VM((1, Z), f32), VM((1, Z), f32),
        VM((2, X, Z), f32), VM((2, Y, Z), f32), VM((2, X, Z), f32),
        VM((STEPS, rows, Z), f32), VM((STEPS, rows, Z), f32), VM((NF, Y, 128), f32),
        VM((N, NF, 128), f32), VM((N, NF, 128), f32), VM((NF, gx_n, 128), f32),
        VM((8, 128), f32), VM((N, 8, 128), f32), VM((BMAX, 512), f32),
        dma((9,)), dma((5,)), dma((STEPS, 6)), dma((STEPS, 6)), dma((2,)), dma((2,)),
        dma((gy_n,)), dma((gy_n,)), dma((2,)), dma((2,)),
    ]
    outs = pl.pallas_call(
        functools.partial(kernel_body, (gx_n, gy_n, X, Y, Z, NB)),
        out_shape=(field, field, field, field, jax.ShapeDtypeStruct((BMAX, 16 * DB), f32)),
        in_specs=[smem] * 6 + [hbm] * 9,
        out_specs=(any_spec,) * 5,
        scratch_shapes=scratch,
        compiler_params=pltpu.CompilerParams(
            collective_id=0, has_side_effects=True, vmem_limit_bytes=60 * 1024 * 1024
        ),
        name="yee",
    )(mask, owner, ieps, dec, drv, res, e, h, jc, pz, mat, line, slots.reshape(1, -1),
      jnp.asarray(vt), jnp.asarray(wt))
    return outs


def solution(mesh):
    field = P(None, "gx", "gy", None)
    in_specs = (
        field, field, field, field, P("gx", "gy", None), P(), P(), P(), P(),
        P(None, "gy"), P(), P("gx", "gy", None), P(),
    )
    out_specs = (field, field, field, field, P(("gx", "gy"), None))
    body = functools.partial(shards, gx_n=mesh.shape["gx"], gy_n=mesh.shape["gy"])
    return jax.shard_map(body, mesh=mesh, in_specs=in_specs, out_specs=out_specs, check_vma=False)
```

```python
import functools
import math

import jax
import jax.numpy as jnp
import numpy as np
from jax import lax
from jax.experimental import pallas as pl
from jax.experimental.pallas import tpu as pltpu
from jax.sharding import PartitionSpec as P

STEPS = 4
NF = 2
DB = 32
BMAX = 4
FREQS = (0.35, 0.6)
WAVENUMS = (0.7, 1.2)
COURANT = 0.5
HIGHEST = lax.Precision.HIGHEST
MESH = pl.DeviceIdType.MESH
PAD = 8


def phase_tables(gx_n, gy_n, cx, cy, total_dirs):
    nu = 64
    nv = total_dirs // nu
    u = (np.arange(nu) + 0.5) / 32.0 - 1.0
    v = (np.arange(nv) + 0.5) * (128.0 / total_dirs) - 1.0
    ys = np.arange(gy_n * cy).reshape(gy_n, cy)
    xs = np.arange(gx_n * cx)
    vt = np.zeros((gy_n, NF, 2 * nv, cy), np.float32)
    wt = np.zeros((NF, gx_n * cx, 2 * nu), np.float32)
    for f, k in enumerate(WAVENUMS):
        ph = k * v[None, :, None] * ys[:, None, :]
        vt[:, f, :nv] = np.cos(ph)
        vt[:, f, nv:] = np.sin(ph)
        pu = k * xs[:, None] * u[None, :]
        wt[f, :, :nu] = np.cos(pu)
        wt[f, :, nu:] = np.sin(pu)
    return vt, wt


def kernel_body(
    dims,
    mask_s,
    owner_s,
    ieps_s,
    dec_s,
    drv_s,
    res_s,
    e_in,
    h_in,
    j_in,
    p_in,
    mat_in,
    line_in,
    slots_in,
    vt_in,
    wt_in,
    e_out,
    h_out,
    j_out,
    p_out,
    far_out,
    e_a, h_a, j_a, p_a, e_b, h_b, j_b, p_b, mat, coef, line_b, line_o, slots, vt, wt,
    xm, xp, ym, yp, ca, cb, ys1, ys0, cas, cbs, hys, gxh, gyh,
    col_e, col_h, ssum, tsend, trecv, tsr, msend, mall, far,
    eh_sem, in_sem, out_sem, snd, rcv, gsnd, grcv, lsnd, lrcv, fsnd, frcv,
):
    GX, GY, X, Y, Z, NB = dims
    N = GX * GY
    V = N
    c = COURANT
    gx = lax.axis_index("gx")
    gy = lax.axis_index("gy")
    me = gx * GY + gy
    e, h, j, p = e_a, h_a, j_a, p_a
    states = ((e_a, h_a, j_a, p_a), (e_b, h_b, j_b, p_b))

    loads = [
        [pltpu.make_async_copy(e_in.at[k], e.at[k, pl.ds(0, X)], eh_sem.at[k]) for k in range(3)],
        [pltpu.make_async_copy(h_in.at[k], h.at[k], eh_sem.at[3 + k]) for k in range(3)],
        pltpu.make_async_copy(line_in, line_o, in_sem.at[2]),
        pltpu.make_async_copy(mat_in, mat, in_sem.at[3]),
        pltpu.make_async_copy(j_in, j, in_sem.at[4]),
        pltpu.make_async_copy(p_in, p, in_sem.at[5]),
        pltpu.make_async_copy(slots_in, slots, in_sem.at[6]),
        pltpu.make_async_copy(vt_in.at[gy], vt, in_sem.at[7]),
        pltpu.make_async_copy(wt_in, wt, in_sem.at[8]),
    ]
    for cp in loads[0] + loads[1] + loads[2:]:
        cp.start()

    has_xm, has_xp = gx > 0, gx < GX - 1
    has_ym, has_yp = gy > 0, gy < GY - 1

    @pl.when(gx == 0)
    def _():
        xm[...] = jnp.zeros_like(xm)
        gxh[...] = jnp.zeros_like(gxh)

    @pl.when(gx == GX - 1)
    def _():
        xp[...] = jnp.zeros_like(xp)

    @pl.when(gy == 0)
    def _():
        ym[...] = jnp.zeros_like(ym)
        gyh[...] = jnp.zeros_like(gyh)

    @pl.when(gy == GY - 1)
    def _():
        yp[...] = jnp.zeros_like(yp)

    @pl.when((gx == 0) | (gy == GY - 1))
    def _():
        ca[...] = jnp.zeros_like(ca)

    @pl.when((gx == GX - 1) | (gy == 0))
    def _():
        cb[...] = jnp.zeros_like(cb)

    for ref in (e_a, e_b):
        for k in (1, 2):
            ref[k, X] = jnp.zeros((Y, Z), jnp.float32)

    barrier = pltpu.get_barrier_semaphore()

    def greet(i, carry):
        d = lax.rem(me + i, N)
        pl.semaphore_signal(barrier, inc=1, device_id=(d // GY, lax.rem(d, GY)), device_id_type=MESH)
        return carry

    lax.fori_loop(1, N, greet, 0)

    for cp in loads[0] + loads[1]:
        cp.wait()

    def pack(x, carry):
        r = pl.ds(x, 1)
        for k in range(3):
            ys1[k, r, :] = e[k, x, pl.ds(Y - 1, 1), :]
        ys0[0, r, :] = e[0, x, pl.ds(0, 1), :]
        ys0[1, r, :] = e[2, x, pl.ds(0, 1), :]
        hys[0, r, :] = h[0, x, pl.ds(Y - 1, 1), :]
        hys[1, r, :] = h[2, x, pl.ds(Y - 1, 1), :]
        return carry

    lax.fori_loop(0, X, pack, 0)
    cas[...] = e[0, X - 1, pl.ds(0, 1), :]
    cbs[...] = e[1, 0, pl.ds(Y - 1, 1), :]
    loads[2].wait()

    pl.semaphore_wait(barrier, N - 1)

    def remote(src, dst, s, r, dx, dy):
        return pltpu.make_async_remote_copy(
            src_ref=src, dst_ref=dst, send_sem=s, recv_sem=r,
            device_id=(gx + dx, gy + dy), device_id_type=MESH,
        )

    def halo(n):
        def cp(src, dst, k, dx, dy):
            return remote(src, dst, snd.at[n, k], rcv.at[n, k], dx, dy)

        return [
            (has_xp, has_xm, cp(states[n % 2][0].at[:, X - 1], xm.at[n], 0, 1, 0)),
            (has_xm, has_xp, cp(states[n % 2][0].at[pl.ds(1, 2), 0], xp.at[n], 1, -1, 0)),
            (has_yp, has_ym, cp(ys1, ym.at[n], 2, 0, 1)),
            (has_ym, has_yp, cp(ys0, yp.at[n], 3, 0, -1)),
            (has_xp & has_ym, has_xm & has_yp, cp(cas, ca.at[n], 4, 1, -1)),
            (has_xm & has_yp, has_xp & has_ym, cp(cbs, cb.at[n], 5, -1, 1)),
        ]

    first_h = [
        (has_xp, has_xm, remote(h.at[pl.ds(1, 2), X - 1], gxh, gsnd.at[0], grcv.at[0], 1, 0)),
        (has_yp, has_ym, remote(hys, gyh, gsnd.at[1], grcv.at[1], 0, 1)),
    ]
    line_cp = []
    for q in range(1, GY):
        dst_gy = lax.rem(gy + q, GY)
        line_cp.append(
            pltpu.make_async_remote_copy(
                src_ref=line_o, dst_ref=line_b.at[gy], send_sem=lsnd.at[q],
                recv_sem=lrcv.at[q], device_id=(gx, dst_gy), device_id_type=MESH,
            )
        )

    def start(copies):
        for to, _, cp in copies:
            pl.when(to)(cp.start)

    def finish(copies):
        for to, frm, cp in copies:
            pl.when(frm)(cp.wait_recv)
            pl.when(to)(cp.wait_send)

    halo0 = halo(0)
    start(halo0)
    start(first_h)
    for cp in line_cp:
        cp.start()
    line_b[gy] = line_o[...]

    lane = lax.broadcasted_iota(jnp.int32, (Y, Z), 1)
    row = lax.broadcasted_iota(jnp.int32, (Y, Z), 0)
    lane_x = lax.broadcasted_iota(jnp.int32, (X, Z), 1)
    row_x = lax.broadcasted_iota(jnp.int32, (X, Z), 0)
    z_h = Z // 4 - 1
    z_e = Z // 4
    z_s = Z // 4 - 3

    loads[3].wait()

    def table(x, carry):
        m = mat[x]
        outs = [jnp.full((Y, Z), t[0], jnp.float32) for t in (ieps_s, dec_s, drv_s, res_s)]
        for k in range(1, 8):
            hit = m == k
            outs = [jnp.where(hit, t[k], o) for t, o in zip((ieps_s, dec_s, drv_s, res_s), outs)]
        for k in range(4):
            coef[k, x] = outs[k]
        return carry

    lax.fori_loop(0, X, table, 0)

    loads[4].wait()
    loads[5].wait()
    for cp in line_cp:
        cp.wait()

    LL = line_o.shape[1]
    R = col_e.shape[1]
    base = gx * X + gy * Y - PAD
    target = 2 * (base + lax.broadcasted_iota(jnp.int32, (R, LL), 0))
    where_l = lax.broadcasted_iota(jnp.int32, (R, LL), 1)
    acc = [jnp.zeros((R, LL), jnp.float32) for _ in range(4)]
    for q in range(GY):
        for par in range(2):
            hit = target + par == where_l + q * LL
            for k in range(2):
                acc[2 * k + par] += jnp.where(hit, line_b[q, pl.ds(k, 1), :], 0.0)
    cols = [jnp.broadcast_to(jnp.sum(a, axis=1, keepdims=True), (R, Z)) for a in acc]
    ev, od, hv, ho = cols
    t2 = 2 * (base + lax.broadcasted_iota(jnp.int32, (R, Z), 0))
    keep_v = ((t2 >= 0) & (t2 < GY * LL)).astype(jnp.float32)
    for n in range(STEPS):
        col_e[n] = od
        ho = (ho - c * (pltpu.roll(ev, R - 1, 0) - od)) * keep_v
        hv = (hv - c * (od - ev)) * keep_v
        col_h[n] = ho
        ev = (ev - c * (hv - pltpu.roll(ho, 1, 0))) * keep_v
        od = (od - c * (ho - hv)) * keep_v

    m_own = mask_s[gy, gx].astype(jnp.float32)
    m_left = mask_s[gy, jnp.maximum(gx - 1, 0)].astype(jnp.float32)
    keep_x = has_xm.astype(jnp.float32)
    keep_y = has_ym.astype(jnp.float32)

    def fz(v, ln):
        return jnp.where(ln == Z - 1, 0.0, pltpu.roll(v, Z - 1, 1)) - v

    def bz(v):
        return v - jnp.where(lane == 0, 0.0, pltpu.roll(v, 1, 1))

    def up_y(v, edge):
        return jnp.where(row == Y - 1, edge, pltpu.roll(v, Y - 1, 0))

    def down_y(v, edge):
        return jnp.where(row == 0, edge, pltpu.roll(v, 1, 0))

    def magnetic(n):
        e, h = states[n % 2][:2]
        h_n = states[(n + 1) % 2][1]

        def body(x, carry):
            ex, ey, ez = e[0, x], e[1, x], e[2, x]
            ey_x, ez_x = e[1, x + 1], e[2, x + 1]
            inj_e = jnp.where(lane == z_h, (c * m_own) * col_e[n, pl.ds(x + PAD, Y), :], 0.0)
            h_n[0, x] = h[0, x] - c * ((up_y(ez, 0.0) - ez) - fz(ey, lane))
            h_n[1, x] = h[1, x] - c * (fz(ex, lane) - (ez_x - ez)) + inj_e
            h_n[2, x] = h[2, x] - c * ((ey_x - ey) - (up_y(ex, 0.0) - ex))
            return carry

        lax.fori_loop(0, X, body, 0, unroll=4)

    def matter(n):
        j, p = states[n % 2][2:]
        e_n, _, j_n, p_n = states[(n + 1) % 2]

        def body(x, carry):
            dc, dr, rs = coef[1, x], coef[2, x], coef[3, x]
            for k in range(3):
                po = p[k, x]
                jn = dc * j[k, x] + dr * e_n[k, x] - rs * po
                j_n[k, x] = jn
                p_n[k, x] = po + jn
            return carry

        lax.fori_loop(0, X, body, 0, unroll=4)

    magnetic(0)
    finish(first_h)
    for n in range(STEPS):
        e, h, j, p = states[n % 2]
        e_n, h_n, j_n, p_n = states[(n + 1) % 2]
        finish(halo0 if n == 0 else pending)
        h_n[1, X - 1] = h_n[1, X - 1] + c * xp[n, 1]
        h_n[2, X - 1] = h_n[2, X - 1] - c * xp[n, 0]
        edge = pl.ds(Y - 1, 1)
        for x in range(X):
            r = pl.ds(x, 1)
            h_n[0, x, edge, :] = h_n[0, x, edge, :] - c * yp[n, 1, r, :]
            h_n[2, x, edge, :] = h_n[2, x, edge, :] + c * yp[n, 0, r, :]
        ex_m, ey_m, ez_m = xm[n, 0], xm[n, 1], xm[n, 2]
        inj = jnp.where(lane == z_h, (c * m_left) * col_e[n, pl.ds(PAD - 1, Y), :], 0.0)
        gh_y = gxh[0] - c * (fz(ex_m, lane) - (e[2, 0] - ez_m)) + inj
        gh_z = gxh[1] - c * ((e[1, 0] - ey_m) - (up_y(ex_m, ca[n]) - ex_m))
        gh_y = gh_y * keep_x
        gh_z = gh_z * keep_x
        gxh[0] = gh_y
        gxh[1] = gh_z
        ex_m, ey_m, ez_m = ym[n, 0], ym[n, 1], ym[n, 2]
        ey_next = jnp.where(row_x == X - 1, cb[n], pltpu.roll(ey_m, X - 1, 0))
        gyh[0] = (gyh[0] - c * ((ys0[1] - ez_m) - fz(ey_m, lane_x))) * keep_y
        gyh[1] = (gyh[1] - c * ((ey_next - ey_m) - (ys0[0] - ex_m))) * keep_y

        def step(x, carry, n=n, e=e, j=j, e_n=e_n, h_n=h_n):
            hy_m, hz_m = carry
            r = pl.ds(x, 1)
            hx, hy, hz = h_n[0, x], h_n[1, x], h_n[2, x]
            inj_h = jnp.where(lane == z_e, m_own * col_h[n, pl.ds(x + PAD, Y), :], 0.0)
            cx = (hz - down_y(hz, gyh[1, r, :])) - bz(hy) + inj_h
            cy = bz(hx) - (hz - hz_m)
            cz = (hy - hy_m) - (hx - down_y(hx, gyh[0, r, :]))
            ie = coef[0, x]
            new = []
            for k, curl in enumerate((cx, cy, cz)):
                en = e[k, x] + ie * (c * curl - j[k, x])
                e_n[k, x] = en
                new.append(en)
            if n < STEPS - 1:
                for k in range(3):
                    ys1[k, r, :] = new[k][Y - 1 : Y]
                ys0[0, r, :] = new[0][0:1]
                ys0[1, r, :] = new[2][0:1]
            return hy, hz

        lax.fori_loop(0, X, step, (gh_y, gh_z), unroll=4)
        if n < STEPS - 1:
            cas[...] = e_n[0, X - 1, pl.ds(0, 1), :]
            cbs[...] = e_n[1, 0, pl.ds(Y - 1, 1), :]
            pending = halo(n + 1)
            start(pending)
        if n == 0:
            loads[6].wait()
            sl = slots[...]
            sl_pos = jnp.maximum(sl, 0)
            sl_x = sl_pos // Y
            sl_y = sl_pos - sl_x * Y
            L = sl.shape[-1]
            one_y = ((lax.broadcasted_iota(jnp.int32, (Y, L), 0) == sl_y) & (sl >= 0)).astype(jnp.bfloat16)
            one_x = (lax.rem(lax.broadcasted_iota(jnp.int32, (128, L), 0), X) == sl_x).astype(jnp.bfloat16)
            cell_mask = lax.dot_general(
                one_y, one_x, (((1,), (1,)), ((), ())), preferred_element_type=jnp.float32
            )
        if n == 1:
            def mine(b, carry):
                cnt, b0, b1, b2, b3 = carry
                hit = owner_s[b] == me
                b0 = jnp.where(hit & (cnt == 0), b, b0)
                b1 = jnp.where(hit & (cnt == 1), b, b1)
                b2 = jnp.where(hit & (cnt == 2), b, b2)
                b3 = jnp.where(hit & (cnt == 3), b, b3)
                return cnt + hit.astype(jnp.int32), b0, b1, b2, b3

            neg = jnp.int32(-1)
            picks = lax.fori_loop(0, NB, mine, (jnp.int32(0), neg, neg, neg, neg))[1:]
        l64 = lax.rem(lane, 4 * X)

        def surface(x, plane, e_n=e_n, h_n=h_n, l64=l64):
            for k, ref in enumerate((e_n.at[0], e_n.at[1], h_n.at[0], h_n.at[1])):
                val = ref[x]
                plane = jnp.where(l64 == k * X + x, val[:, z_s : z_s + 1], plane)
            return plane

        plane = lax.fori_loop(0, X, surface, jnp.zeros((Y, Z), jnp.float32), unroll=4)
        for f in range(NF):
            wc = math.cos(FREQS[f] * (n + 1))
            ws = -math.sin(FREQS[f] * (n + 1))
            add = jnp.where(lane < 4 * X, wc, ws) * plane
            ssum[f] = add if n == 0 else ssum[f] + add

        if n < STEPS - 1:
            matter(n)
            magnetic(n + 1)
    e, h, j, p = states[STEPS % 2]
    stores = [
        pltpu.make_async_copy(e.at[:, pl.ds(0, X)], e_out, out_sem.at[0]),
        pltpu.make_async_copy(h, h_out, out_sem.at[1]),
        pltpu.make_async_copy(j, j_out, out_sem.at[2]),
        pltpu.make_async_copy(p, p_out, out_sem.at[3]),
    ]
    stores[0].start()
    stores[1].start()

    loads[7].wait()
    loads[8].wait()
    lane_v = lax.broadcasted_iota(jnp.int32, (V, 128), 1)
    for f in range(NF):
        cd = jnp.dot(vt[f], ssum[f] * cell_mask, precision=HIGHEST, preferred_element_type=jnp.float32)
        turned = pltpu.roll(cd[V:], 64, 1)
        t = cd[:V] + jnp.where(lane_v < 64, -turned, turned)
        for v in range(V):
            tsend[v, pl.ds(f, 1), :] = t[v : v + 1]

    def send_t(i, carry):
        d = lax.rem(me + i, N)
        pltpu.make_async_remote_copy(
            src_ref=tsend.at[d], dst_ref=trecv.at[me], send_sem=fsnd.at[0], recv_sem=frcv.at[0],
            device_id=(d // GY, lax.rem(d, GY)), device_id_type=MESH,
        ).start()
        return carry

    lax.fori_loop(1, N, send_t, 0)
    matter(STEPS - 1)
    stores[2].start()
    stores[3].start()
    trecv[me] = tsend[me]
    part = pl.ds(0, N - 1)
    pltpu.make_async_copy(trecv.at[part], trecv.at[part], frcv.at[0]).wait()

    for q in range(GX):
        total = trecv[q * GY]
        for s in range(1, GY):
            total = total + trecv[q * GY + s]
        for f in range(NF):
            tsr[f, pl.ds(q, 1), :] = total[f : f + 1]

    l8 = lax.broadcasted_iota(jnp.int32, (8, 128), 1)
    r8 = lax.broadcasted_iota(jnp.int32, (8, 128), 0)
    blk = l8 // X
    grp = l8 // 32
    rows_out = [None] * 8
    for f in range(NF):
        g = jnp.zeros((8, 128), jnp.float32)
        for o in range(GX // 8):
            a = tsr[f, pl.ds(8 * o, 8), :]
            for s in (4, 2, 1):
                from_down = pltpu.roll(pltpu.roll(a, 8 - s, 0), X * s, 1)
                from_up = pltpu.roll(pltpu.roll(a, s, 0), 128 - X * s, 1)
                bi = (r8 & s) != 0
                bj = (blk & s) != 0
                a = jnp.where(bi == bj, a, jnp.where(bj, from_down, from_up))
            g = g + jnp.dot(a, wt[f, pl.ds(o * 128, 128), :], precision=HIGHEST,
                            preferred_element_type=jnp.float32)
        for hh in range(2):
            rep = []
            for cs in range(2):
                w = jnp.where(grp == cs * 2 + hh, g, 0.0)
                w = w + pltpu.roll(w, 32, 1)
                rep.append(w + pltpu.roll(w, 64, 1))
            for chi in range(2):
                comp = chi * 2 + grp // 2
                part_b = grp & 1
                same = r8 == part_b * 4 + comp
                other = r8 == (1 - part_b) * 4 + comp
                sgn = jnp.where(part_b == 1, 1.0, -1.0)
                mix = jnp.where(same, rep[0], 0.0) + jnp.where(other, sgn * rep[1], 0.0)
                rows_out[hh * 4 + f * 2 + chi] = jnp.sum(mix, axis=0, keepdims=True)
    scale = 1.0 / math.sqrt(N * L)
    for i in range(8):
        msend[pl.ds(i, 1), :] = rows_out[i] * scale

    def send_m(i, carry):
        d = lax.rem(me + i, N)
        pltpu.make_async_remote_copy(
            src_ref=msend, dst_ref=mall.at[me], send_sem=fsnd.at[1], recv_sem=frcv.at[1],
            device_id=(d // GY, lax.rem(d, GY)), device_id_type=MESH,
        ).start()
        return carry

    lax.fori_loop(1, N, send_m, 0)
    mall[me] = msend[...]
    pltpu.make_async_copy(mall.at[part], mall.at[part], frcv.at[1]).wait()
    for r in range(BMAX):
        b = picks[r]
        ok = (b >= 0).astype(jnp.float32)
        bb = jnp.maximum(b, 0)
        tile = mall[bb // 2] * ok
        half = jnp.where(lax.rem(bb, 2) == 1, tile[4:8], tile[0:4])
        for k in range(4):
            far[pl.ds(r, 1), pl.ds(k * 128, 128)] = half[k : k + 1]
    last = pltpu.make_async_copy(far, far_out, out_sem.at[4])
    last.start()
    pltpu.make_async_copy(tsend.at[part], tsend.at[part], fsnd.at[0]).wait()
    pltpu.make_async_copy(mall.at[part], mall.at[part], fsnd.at[1]).wait()
    for cp in stores:
        cp.wait()
    last.wait()


def write_body(*refs):
    bufs, (far_b, s_in, s_out) = refs[10:14], refs[14:]
    far_load = pltpu.make_async_copy(refs[4], far_b, s_in.at[4, 0])
    far_store = pltpu.make_async_copy(far_b, refs[9], s_out.at[4, 0])
    loads, stores = [], []
    for i in range(4):
        for k in range(3):
            loads.append(pltpu.make_async_copy(refs[i].at[k], bufs[i].at[k], s_in.at[i, k]))
            stores.append(pltpu.make_async_copy(bufs[i].at[k], refs[5 + i].at[k], s_out.at[i, k]))
    loads.append(far_load)
    stores.append(far_store)
    for cp in loads:
        cp.start()
    for a, b in zip(loads, stores):
        a.wait()
        b.start()
    for cp in stores:
        cp.wait()


def shards(e, h, jc, pz, mat, ieps, dec, drv, res, line, mask, slots, owner, gx_n=0, gy_n=0):
    _, X, Y, Z = e.shape
    N = gx_n * gy_n
    NB = owner.shape[0]
    vt, wt = phase_tables(gx_n, gy_n, X, Y, NB * DB)
    f32 = jnp.float32
    any_spec = pl.BlockSpec(memory_space=pl.ANY)
    hbm = pl.BlockSpec(memory_space=pltpu.HBM)
    smem = pl.BlockSpec(memory_space=pltpu.SMEM)
    field = jax.ShapeDtypeStruct((3, X, Y, Z), f32)
    rows = X + Y + 2 * PAD
    VM = pltpu.VMEM
    dma = pltpu.SemaphoreType.DMA
    scratch = [
        VM((3, X + 1, Y, Z), f32), VM((3, X, Y, Z), f32), VM((3, X, Y, Z), f32),
        VM((3, X, Y, Z), f32), VM((3, X + 1, Y, Z), f32), VM((3, X, Y, Z), f32),
        VM((3, X, Y, Z), f32), VM((3, X, Y, Z), f32), VM((X, Y, Z), jnp.int32), VM((4, X, Y, Z), f32),
        VM((gy_n,) + line.shape, f32), VM(line.shape, f32), VM((1, slots.shape[-1]), jnp.int32),
        VM(vt.shape[1:], f32), VM(wt.shape, f32),
        VM((STEPS, 3, Y, Z), f32), VM((STEPS, 2, Y, Z), f32), VM((STEPS, 3, X, Z), f32),
        VM((STEPS, 2, X, Z), f32), VM((STEPS, 1, Z), f32), VM((STEPS, 1, Z), f32),
        VM((3, X, Z), f32), VM((2, X, Z), f32), VM((1, Z), f32), VM((1, Z), f32),
        VM((2, X, Z), f32), VM((2, Y, Z), f32), VM((2, X, Z), f32),
        VM((STEPS, rows, Z), f32), VM((STEPS, rows, Z), f32), VM((NF, Y, 128), f32),
        VM((N, NF, 128), f32), VM((N, NF, 128), f32), VM((NF, gx_n, 128), f32),
        VM((8, 128), f32), VM((N, 8, 128), f32), VM((BMAX, 512), f32),
        dma((6,)), dma((9,)), dma((5,)), dma((STEPS, 6)), dma((STEPS, 6)), dma((2,)), dma((2,)),
        dma((gy_n,)), dma((gy_n,)), dma((2,)), dma((2,)),
    ]
    outs = pl.pallas_call(
        functools.partial(kernel_body, (gx_n, gy_n, X, Y, Z, NB)),
        out_shape=(field, field, field, field, jax.ShapeDtypeStruct((BMAX, 16 * DB), f32)),
        in_specs=[smem] * 6 + [hbm] * 9,
        out_specs=(any_spec,) * 5,
        scratch_shapes=scratch,
        compiler_params=pltpu.CompilerParams(
            collective_id=0, has_side_effects=True, vmem_limit_bytes=60 * 1024 * 1024
        ),
        name="yee",
    )(mask.T, owner, ieps, dec, drv, res, e, h, jc, pz, mat, line, slots.reshape(1, -1),
      jnp.asarray(vt), jnp.asarray(wt))
    bufs = [VM((3, X, Y, Z), f32)] * 4
    return pl.pallas_call(
        write_body,
        out_shape=tuple(jax.ShapeDtypeStruct(o.shape, o.dtype) for o in outs),
        in_specs=[any_spec] * 5,
        out_specs=(any_spec,) * 5,
        scratch_shapes=bufs + [VM((BMAX, 16 * DB), f32), dma((5, 3)), dma((5, 3))],
        compiler_params=pltpu.CompilerParams(vmem_limit_bytes=60 * 1024 * 1024),
        name="write",
    )(*outs)


def solution(mesh):
    field = P(None, "gx", "gy", None)
    in_specs = (
        field, field, field, field, P("gx", "gy", None), P(), P(), P(), P(),
        P(None, "gy"), P(), P("gx", "gy", None), P(),
    )
    out_specs = (field, field, field, field, P(("gx", "gy"), None))
    body = functools.partial(shards, gx_n=mesh.shape["gx"], gy_n=mesh.shape["gy"])
    return jax.shard_map(body, mesh=mesh, in_specs=in_specs, out_specs=out_specs, check_vma=False)
```

```python
import functools
import math

import jax
import jax.numpy as jnp
import numpy as np
from jax import lax
from jax.experimental import pallas as pl
from jax.experimental.pallas import tpu as pltpu
from jax.sharding import PartitionSpec as P

STEPS = 4
NF = 2
DB = 32
BMAX = 4
FREQS = (0.35, 0.6)
WAVENUMS = (0.7, 1.2)
COURANT = 0.5
HIGHEST = lax.Precision.HIGHEST
MESH = pl.DeviceIdType.MESH
PAD = 8


def phase_tables(gx_n, gy_n, cx, cy, total_dirs):
    nu = 64
    nv = total_dirs // nu
    u = (np.arange(nu) + 0.5) / 32.0 - 1.0
    v = (np.arange(nv) + 0.5) * (128.0 / total_dirs) - 1.0
    ys = np.arange(gy_n * cy).reshape(gy_n, cy)
    xs = np.arange(gx_n * cx)
    vt = np.zeros((gy_n, NF, 2 * nv, cy), np.float32)
    wt = np.zeros((NF, gx_n * cx, 2 * nu), np.float32)
    for f, k in enumerate(WAVENUMS):
        ph = k * v[None, :, None] * ys[:, None, :]
        vt[:, f, :nv] = np.cos(ph)
        vt[:, f, nv:] = np.sin(ph)
        pu = k * xs[:, None] * u[None, :]
        wt[f, :, :nu] = np.cos(pu)
        wt[f, :, nu:] = np.sin(pu)
    return vt, wt


def kernel_body(
    dims,
    mask_s,
    owner_s,
    ieps_s,
    dec_s,
    drv_s,
    res_s,
    e_in,
    h_in,
    j_in,
    p_in,
    mat_in,
    line_in,
    slots_in,
    vt_in,
    wt_in,
    e_out,
    h_out,
    j_out,
    p_out,
    far_out,
    e_a, h_a, j_a, p_a, e_b, h_b, j_b, p_b, mat, coef, line_b, line_o, slots, vt, wt,
    xm, xp, ym, yp, ca, cb, ys1, ys0, cas, cbs, hys, gxh, gyh,
    col_e, col_h, ssum, tsend, trecv, tsr, msend, mall, far,
    eh_sem, in_sem, out_sem, snd, rcv, gsnd, grcv, lsnd, lrcv, fsnd, frcv,
):
    GX, GY, X, Y, Z, NB = dims
    N = GX * GY
    V = N
    c = COURANT
    gx = lax.axis_index("gx")
    gy = lax.axis_index("gy")
    me = gx * GY + gy
    e, h, j, p = e_a, h_a, j_a, p_a
    states = ((e_a, h_a, j_a, p_a), (e_b, h_b, j_b, p_b))

    loads = [
        [pltpu.make_async_copy(e_in.at[k], e.at[k, pl.ds(0, X)], eh_sem.at[k]) for k in range(3)],
        [pltpu.make_async_copy(h_in.at[k], h.at[k], eh_sem.at[3 + k]) for k in range(3)],
        pltpu.make_async_copy(line_in, line_o, in_sem.at[2]),
        pltpu.make_async_copy(mat_in, mat, in_sem.at[3]),
        pltpu.make_async_copy(j_in, j, in_sem.at[4]),
        pltpu.make_async_copy(p_in, p, in_sem.at[5]),
        pltpu.make_async_copy(slots_in, slots, in_sem.at[6]),
        pltpu.make_async_copy(vt_in.at[gy], vt, in_sem.at[7]),
        pltpu.make_async_copy(wt_in, wt, in_sem.at[8]),
    ]
    for cp in loads[0] + loads[1] + loads[2:4]:
        cp.start()

    has_xm, has_xp = gx > 0, gx < GX - 1
    has_ym, has_yp = gy > 0, gy < GY - 1

    @pl.when(gx == 0)
    def _():
        xm[...] = jnp.zeros_like(xm)
        gxh[...] = jnp.zeros_like(gxh)

    @pl.when(gx == GX - 1)
    def _():
        xp[...] = jnp.zeros_like(xp)

    @pl.when(gy == 0)
    def _():
        ym[...] = jnp.zeros_like(ym)
        gyh[...] = jnp.zeros_like(gyh)

    @pl.when(gy == GY - 1)
    def _():
        yp[...] = jnp.zeros_like(yp)

    @pl.when((gx == 0) | (gy == GY - 1))
    def _():
        ca[...] = jnp.zeros_like(ca)

    @pl.when((gx == GX - 1) | (gy == 0))
    def _():
        cb[...] = jnp.zeros_like(cb)

    for ref in (e_a, e_b):
        for k in (1, 2):
            ref[k, X] = jnp.zeros((Y, Z), jnp.float32)

    barrier = pltpu.get_barrier_semaphore()

    def greet(i, carry):
        d = lax.rem(me + i, N)
        pl.semaphore_signal(barrier, inc=1, device_id=(d // GY, lax.rem(d, GY)), device_id_type=MESH)
        return carry

    lax.fori_loop(1, N, greet, 0)

    for cp in loads[0] + loads[1]:
        cp.wait()
    for cp in loads[4:]:
        cp.start()

    def pack(x, carry):
        r = pl.ds(x, 1)
        for k in range(3):
            ys1[k, r, :] = e[k, x, pl.ds(Y - 1, 1), :]
        ys0[0, r, :] = e[0, x, pl.ds(0, 1), :]
        ys0[1, r, :] = e[2, x, pl.ds(0, 1), :]
        hys[0, r, :] = h[0, x, pl.ds(Y - 1, 1), :]
        hys[1, r, :] = h[2, x, pl.ds(Y - 1, 1), :]
        return carry

    lax.fori_loop(0, X, pack, 0, unroll=4)
    cas[...] = e[0, X - 1, pl.ds(0, 1), :]
    cbs[...] = e[1, 0, pl.ds(Y - 1, 1), :]
    loads[2].wait()

    pl.semaphore_wait(barrier, N - 1)

    def remote(src, dst, s, r, dx, dy):
        return pltpu.make_async_remote_copy(
            src_ref=src, dst_ref=dst, send_sem=s, recv_sem=r,
            device_id=(gx + dx, gy + dy), device_id_type=MESH,
        )

    def halo(n):
        def cp(src, dst, k, dx, dy):
            return remote(src, dst, snd.at[n, k], rcv.at[n, k], dx, dy)

        return [
            (has_xp, has_xm, cp(states[n % 2][0].at[:, X - 1], xm.at[n], 0, 1, 0)),
            (has_xm, has_xp, cp(states[n % 2][0].at[pl.ds(1, 2), 0], xp.at[n], 1, -1, 0)),
            (has_yp, has_ym, cp(ys1, ym.at[n], 2, 0, 1)),
            (has_ym, has_yp, cp(ys0, yp.at[n], 3, 0, -1)),
            (has_xp & has_ym, has_xm & has_yp, cp(cas, ca.at[n], 4, 1, -1)),
            (has_xm & has_yp, has_xp & has_ym, cp(cbs, cb.at[n], 5, -1, 1)),
        ]

    first_h = [
        (has_xp, has_xm, remote(h.at[pl.ds(1, 2), X - 1], gxh, gsnd.at[0], grcv.at[0], 1, 0)),
        (has_yp, has_ym, remote(hys, gyh, gsnd.at[1], grcv.at[1], 0, 1)),
    ]
    line_cp = []
    for q in range(1, GY):
        dst_gy = lax.rem(gy + q, GY)
        line_cp.append(
            pltpu.make_async_remote_copy(
                src_ref=line_o, dst_ref=line_b.at[gy], send_sem=lsnd.at[q],
                recv_sem=lrcv.at[q], device_id=(gx, dst_gy), device_id_type=MESH,
            )
        )

    def start(copies):
        for to, _, cp in copies:
            pl.when(to)(cp.start)

    def finish(copies):
        for to, frm, cp in copies:
            pl.when(frm)(cp.wait_recv)
            pl.when(to)(cp.wait_send)

    halo0 = halo(0)
    start(halo0)
    start(first_h)
    for cp in line_cp:
        cp.start()
    line_b[gy] = line_o[...]

    lane = lax.broadcasted_iota(jnp.int32, (Y, Z), 1)
    row = lax.broadcasted_iota(jnp.int32, (Y, Z), 0)
    lane_x = lax.broadcasted_iota(jnp.int32, (X, Z), 1)
    row_x = lax.broadcasted_iota(jnp.int32, (X, Z), 0)
    z_h = Z // 4 - 1
    z_e = Z // 4
    z_s = Z // 4 - 3

    loads[3].wait()

    def table(x, carry):
        m = mat[x]
        outs = [jnp.full((Y, Z), t[0], jnp.float32) for t in (ieps_s, dec_s, drv_s, res_s)]
        for k in range(1, 8):
            hit = m == k
            outs = [jnp.where(hit, t[k], o) for t, o in zip((ieps_s, dec_s, drv_s, res_s), outs)]
        for k in range(4):
            coef[k, x] = outs[k]
        return carry

    lax.fori_loop(0, X, table, 0, unroll=2)

    loads[4].wait()
    loads[5].wait()
    for cp in line_cp:
        cp.wait()

    LL = line_o.shape[1]
    R = col_e.shape[1]
    base = gx * X + gy * Y - PAD
    target = 2 * (base + lax.broadcasted_iota(jnp.int32, (R, LL), 0))
    where_l = lax.broadcasted_iota(jnp.int32, (R, LL), 1)
    acc = [jnp.zeros((R, LL), jnp.float32) for _ in range(4)]
    for q in range(GY):
        for par in range(2):
            hit = target + par == where_l + q * LL
            for k in range(2):
                acc[2 * k + par] += jnp.where(hit, line_b[q, pl.ds(k, 1), :], 0.0)
    cols = [jnp.broadcast_to(jnp.sum(a, axis=1, keepdims=True), (R, Z)) for a in acc]
    ev, od, hv, ho = cols
    t2 = 2 * (base + lax.broadcasted_iota(jnp.int32, (R, Z), 0))
    keep_v = ((t2 >= 0) & (t2 < GY * LL)).astype(jnp.float32)
    for n in range(STEPS):
        col_e[n] = od
        ho = (ho - c * (pltpu.roll(ev, R - 1, 0) - od)) * keep_v
        hv = (hv - c * (od - ev)) * keep_v
        col_h[n] = ho
        ev = (ev - c * (hv - pltpu.roll(ho, 1, 0))) * keep_v
        od = (od - c * (ho - hv)) * keep_v

    m_own = mask_s[gy, gx].astype(jnp.float32)
    m_left = mask_s[gy, jnp.maximum(gx - 1, 0)].astype(jnp.float32)
    keep_x = has_xm.astype(jnp.float32)
    keep_y = has_ym.astype(jnp.float32)

    def fz(v, ln):
        return jnp.where(ln == Z - 1, 0.0, pltpu.roll(v, Z - 1, 1)) - v

    def bz(v):
        return v - jnp.where(lane == 0, 0.0, pltpu.roll(v, 1, 1))

    def up_y(v, edge):
        return jnp.where(row == Y - 1, edge, pltpu.roll(v, Y - 1, 0))

    def down_y(v, edge):
        return jnp.where(row == 0, edge, pltpu.roll(v, 1, 0))

    def magnetic(n):
        e, h = states[n % 2][:2]
        h_n = states[(n + 1) % 2][1]

        def body(x, carry):
            ex, ey, ez = e[0, x], e[1, x], e[2, x]
            ey_x, ez_x = e[1, x + 1], e[2, x + 1]
            inj_e = jnp.where(lane == z_h, (c * m_own) * col_e[n, pl.ds(x + PAD, Y), :], 0.0)
            h_n[0, x] = h[0, x] - c * ((up_y(ez, 0.0) - ez) - fz(ey, lane))
            h_n[1, x] = h[1, x] - c * (fz(ex, lane) - (ez_x - ez)) + inj_e
            h_n[2, x] = h[2, x] - c * ((ey_x - ey) - (up_y(ex, 0.0) - ex))
            return carry

        lax.fori_loop(0, X, body, 0, unroll=4)

    def matter(n):
        j, p = states[n % 2][2:]
        e_n, _, j_n, p_n = states[(n + 1) % 2]

        def body(x, carry):
            dc, dr, rs = coef[1, x], coef[2, x], coef[3, x]
            for k in range(3):
                po = p[k, x]
                jn = dc * j[k, x] + dr * e_n[k, x] - rs * po
                j_n[k, x] = jn
                p_n[k, x] = po + jn
            return carry

        lax.fori_loop(0, X, body, 0, unroll=4)

    magnetic(0)
    finish(first_h)
    for n in range(STEPS):
        e, h, j, p = states[n % 2]
        e_n, h_n, j_n, p_n = states[(n + 1) % 2]
        finish(halo0 if n == 0 else pending)
        h_n[1, X - 1] = h_n[1, X - 1] + c * xp[n, 1]
        h_n[2, X - 1] = h_n[2, X - 1] - c * xp[n, 0]
        edge = pl.ds(Y - 1, 1)
        for x in range(X):
            r = pl.ds(x, 1)
            h_n[0, x, edge, :] = h_n[0, x, edge, :] - c * yp[n, 1, r, :]
            h_n[2, x, edge, :] = h_n[2, x, edge, :] + c * yp[n, 0, r, :]
        ex_m, ey_m, ez_m = xm[n, 0], xm[n, 1], xm[n, 2]
        inj = jnp.where(lane == z_h, (c * m_left) * col_e[n, pl.ds(PAD - 1, Y), :], 0.0)
        gh_y = gxh[0] - c * (fz(ex_m, lane) - (e[2, 0] - ez_m)) + inj
        gh_z = gxh[1] - c * ((e[1, 0] - ey_m) - (up_y(ex_m, ca[n]) - ex_m))
        gh_y = gh_y * keep_x
        gh_z = gh_z * keep_x
        gxh[0] = gh_y
        gxh[1] = gh_z
        ex_m, ey_m, ez_m = ym[n, 0], ym[n, 1], ym[n, 2]
        ey_next = jnp.where(row_x == X - 1, cb[n], pltpu.roll(ey_m, X - 1, 0))
        gyh[0] = (gyh[0] - c * ((ys0[1] - ez_m) - fz(ey_m, lane_x))) * keep_y
        gyh[1] = (gyh[1] - c * ((ey_next - ey_m) - (ys0[0] - ex_m))) * keep_y

        def step(x, carry, n=n, e=e, j=j, e_n=e_n, h_n=h_n):
            hy_m, hz_m = carry
            r = pl.ds(x, 1)
            hx, hy, hz = h_n[0, x], h_n[1, x], h_n[2, x]
            inj_h = jnp.where(lane == z_e, m_own * col_h[n, pl.ds(x + PAD, Y), :], 0.0)
            cx = (hz - down_y(hz, gyh[1, r, :])) - bz(hy) + inj_h
            cy = bz(hx) - (hz - hz_m)
            cz = (hy - hy_m) - (hx - down_y(hx, gyh[0, r, :]))
            ie = coef[0, x]
            new = []
            for k, curl in enumerate((cx, cy, cz)):
                en = e[k, x] + ie * (c * curl - j[k, x])
                e_n[k, x] = en
                new.append(en)
            if n < STEPS - 1:
                for k in range(3):
                    ys1[k, r, :] = new[k][Y - 1 : Y]
                ys0[0, r, :] = new[0][0:1]
                ys0[1, r, :] = new[2][0:1]
            return hy, hz

        lax.fori_loop(0, X, step, (gh_y, gh_z), unroll=8)
        if n < STEPS - 1:
            cas[...] = e_n[0, X - 1, pl.ds(0, 1), :]
            cbs[...] = e_n[1, 0, pl.ds(Y - 1, 1), :]
            pending = halo(n + 1)
            start(pending)
        if n == 0:
            loads[6].wait()
            sl = slots[...]
            sl_pos = jnp.maximum(sl, 0)
            sl_x = sl_pos // Y
            sl_y = sl_pos - sl_x * Y
            L = sl.shape[-1]
            one_y = ((lax.broadcasted_iota(jnp.int32, (Y, L), 0) == sl_y) & (sl >= 0)).astype(jnp.bfloat16)
            one_x = (lax.rem(lax.broadcasted_iota(jnp.int32, (128, L), 0), X) == sl_x).astype(jnp.bfloat16)
            cell_mask = lax.dot_general(
                one_y, one_x, (((1,), (1,)), ((), ())), preferred_element_type=jnp.float32
            )
        if n == 1:
            def mine(b, carry):
                cnt, b0, b1, b2, b3 = carry
                hit = owner_s[b] == me
                b0 = jnp.where(hit & (cnt == 0), b, b0)
                b1 = jnp.where(hit & (cnt == 1), b, b1)
                b2 = jnp.where(hit & (cnt == 2), b, b2)
                b3 = jnp.where(hit & (cnt == 3), b, b3)
                return cnt + hit.astype(jnp.int32), b0, b1, b2, b3

            neg = jnp.int32(-1)
            picks = lax.fori_loop(0, NB, mine, (jnp.int32(0), neg, neg, neg, neg))[1:]
        l64 = lax.rem(lane, 4 * X)

        def surface(x, plane, e_n=e_n, h_n=h_n, l64=l64):
            for k, ref in enumerate((e_n.at[0], e_n.at[1], h_n.at[0], h_n.at[1])):
                val = ref[x]
                plane = jnp.where(l64 == k * X + x, val[:, z_s : z_s + 1], plane)
            return plane

        plane = lax.fori_loop(0, X, surface, jnp.zeros((Y, Z), jnp.float32), unroll=4)
        for f in range(NF):
            wc = math.cos(FREQS[f] * (n + 1))
            ws = -math.sin(FREQS[f] * (n + 1))
            add = jnp.where(lane < 4 * X, wc, ws) * plane
            ssum[f] = add if n == 0 else ssum[f] + add

        if n < STEPS - 1:
            matter(n)
            magnetic(n + 1)
    e, h, j, p = states[STEPS % 2]
    stores = [
        pltpu.make_async_copy(e.at[:, pl.ds(0, X)], e_out, out_sem.at[0]),
        pltpu.make_async_copy(h, h_out, out_sem.at[1]),
        pltpu.make_async_copy(j, j_out, out_sem.at[2]),
        pltpu.make_async_copy(p, p_out, out_sem.at[3]),
    ]
    stores[0].start()
    stores[1].start()

    loads[7].wait()
    loads[8].wait()
    lane_v = lax.broadcasted_iota(jnp.int32, (V, 128), 1)
    for f in range(NF):
        cd = jnp.dot(vt[f], ssum[f] * cell_mask, precision=HIGHEST, preferred_element_type=jnp.float32)
        turned = pltpu.roll(cd[V:], 64, 1)
        t = cd[:V] + jnp.where(lane_v < 64, -turned, turned)
        for v in range(V):
            tsend[v, pl.ds(f, 1), :] = t[v : v + 1]

    def send_t(i, carry):
        d = lax.rem(me + i, N)
        pltpu.make_async_remote_copy(
            src_ref=tsend.at[d], dst_ref=trecv.at[me], send_sem=fsnd.at[0], recv_sem=frcv.at[0],
            device_id=(d // GY, lax.rem(d, GY)), device_id_type=MESH,
        ).start()
        return carry

    lax.fori_loop(1, N, send_t, 0)
    matter(STEPS - 1)
    stores[2].start()
    stores[3].start()
    trecv[me] = tsend[me]
    part = pl.ds(0, N - 1)
    pltpu.make_async_copy(trecv.at[part], trecv.at[part], frcv.at[0]).wait()

    for q in range(GX):
        total = trecv[q * GY]
        for s in range(1, GY):
            total = total + trecv[q * GY + s]
        for f in range(NF):
            tsr[f, pl.ds(q, 1), :] = total[f : f + 1]

    l8 = lax.broadcasted_iota(jnp.int32, (8, 128), 1)
    r8 = lax.broadcasted_iota(jnp.int32, (8, 128), 0)
    blk = l8 // X
    grp = l8 // 32
    rows_out = [None] * 8
    for f in range(NF):
        g = jnp.zeros((8, 128), jnp.float32)
        for o in range(GX // 8):
            a = tsr[f, pl.ds(8 * o, 8), :]
            for s in (4, 2, 1):
                from_down = pltpu.roll(pltpu.roll(a, 8 - s, 0), X * s, 1)
                from_up = pltpu.roll(pltpu.roll(a, s, 0), 128 - X * s, 1)
                bi = (r8 & s) != 0
                bj = (blk & s) != 0
                a = jnp.where(bi == bj, a, jnp.where(bj, from_down, from_up))
            g = g + jnp.dot(a, wt[f, pl.ds(o * 128, 128), :], precision=HIGHEST,
                            preferred_element_type=jnp.float32)
        for hh in range(2):
            rep = []
            for cs in range(2):
                w = jnp.where(grp == cs * 2 + hh, g, 0.0)
                w = w + pltpu.roll(w, 32, 1)
                rep.append(w + pltpu.roll(w, 64, 1))
            for chi in range(2):
                comp = chi * 2 + grp // 2
                part_b = grp & 1
                same = r8 == part_b * 4 + comp
                other = r8 == (1 - part_b) * 4 + comp
                sgn = jnp.where(part_b == 1, 1.0, -1.0)
                mix = jnp.where(same, rep[0], 0.0) + jnp.where(other, sgn * rep[1], 0.0)
                rows_out[hh * 4 + f * 2 + chi] = jnp.sum(mix, axis=0, keepdims=True)
    scale = 1.0 / math.sqrt(N * L)
    for i in range(8):
        msend[pl.ds(i, 1), :] = rows_out[i] * scale

    def send_m(i, carry):
        d = lax.rem(me + i, N)
        pltpu.make_async_remote_copy(
            src_ref=msend, dst_ref=mall.at[me], send_sem=fsnd.at[1], recv_sem=frcv.at[1],
            device_id=(d // GY, lax.rem(d, GY)), device_id_type=MESH,
        ).start()
        return carry

    lax.fori_loop(1, N, send_m, 0)
    mall[me] = msend[...]
    pltpu.make_async_copy(mall.at[part], mall.at[part], frcv.at[1]).wait()
    for r in range(BMAX):
        b = picks[r]
        ok = (b >= 0).astype(jnp.float32)
        bb = jnp.maximum(b, 0)
        tile = mall[bb // 2] * ok
        half = jnp.where(lax.rem(bb, 2) == 1, tile[4:8], tile[0:4])
        for k in range(4):
            far[pl.ds(r, 1), pl.ds(k * 128, 128)] = half[k : k + 1]
    last = pltpu.make_async_copy(far, far_out, out_sem.at[4])
    last.start()
    pltpu.make_async_copy(tsend.at[part], tsend.at[part], fsnd.at[0]).wait()
    pltpu.make_async_copy(mall.at[part], mall.at[part], fsnd.at[1]).wait()
    for cp in stores:
        cp.wait()
    last.wait()


def write_body(*refs):
    bufs, (far_b, s_in, s_out) = refs[10:14], refs[14:]
    far_load = pltpu.make_async_copy(refs[4], far_b, s_in.at[4, 0])
    far_store = pltpu.make_async_copy(far_b, refs[9], s_out.at[4, 0])
    loads, stores = [], []
    for i in range(4):
        for k in range(3):
            loads.append(pltpu.make_async_copy(refs[i].at[k], bufs[i].at[k], s_in.at[i, k]))
            stores.append(pltpu.make_async_copy(bufs[i].at[k], refs[5 + i].at[k], s_out.at[i, k]))
    loads.append(far_load)
    stores.append(far_store)
    for cp in loads:
        cp.start()
    for a, b in zip(loads, stores):
        a.wait()
        b.start()
    for cp in stores:
        cp.wait()


def shards(e, h, jc, pz, mat, ieps, dec, drv, res, line, mask, slots, owner, gx_n=0, gy_n=0):
    _, X, Y, Z = e.shape
    N = gx_n * gy_n
    NB = owner.shape[0]
    vt, wt = phase_tables(gx_n, gy_n, X, Y, NB * DB)
    f32 = jnp.float32
    any_spec = pl.BlockSpec(memory_space=pl.ANY)
    hbm = pl.BlockSpec(memory_space=pltpu.HBM)
    smem = pl.BlockSpec(memory_space=pltpu.SMEM)
    field = jax.ShapeDtypeStruct((3, X, Y, Z), f32)
    rows = X + Y + 2 * PAD
    VM = pltpu.VMEM
    dma = pltpu.SemaphoreType.DMA
    scratch = [
        VM((3, X + 1, Y, Z), f32), VM((3, X, Y, Z), f32), VM((3, X, Y, Z), f32),
        VM((3, X, Y, Z), f32), VM((3, X + 1, Y, Z), f32), VM((3, X, Y, Z), f32),
        VM((3, X, Y, Z), f32), VM((3, X, Y, Z), f32), VM((X, Y, Z), jnp.int32), VM((4, X, Y, Z), f32),
        VM((gy_n,) + line.shape, f32), VM(line.shape, f32), VM((1, slots.shape[-1]), jnp.int32),
        VM(vt.shape[1:], f32), VM(wt.shape, f32),
        VM((STEPS, 3, Y, Z), f32), VM((STEPS, 2, Y, Z), f32), VM((STEPS, 3, X, Z), f32),
        VM((STEPS, 2, X, Z), f32), VM((STEPS, 1, Z), f32), VM((STEPS, 1, Z), f32),
        VM((3, X, Z), f32), VM((2, X, Z), f32), VM((1, Z), f32), VM((1, Z), f32),
        VM((2, X, Z), f32), VM((2, Y, Z), f32), VM((2, X, Z), f32),
        VM((STEPS, rows, Z), f32), VM((STEPS, rows, Z), f32), VM((NF, Y, 128), f32),
        VM((N, NF, 128), f32), VM((N, NF, 128), f32), VM((NF, gx_n, 128), f32),
        VM((8, 128), f32), VM((N, 8, 128), f32), VM((BMAX, 512), f32),
        dma((6,)), dma((9,)), dma((5,)), dma((STEPS, 6)), dma((STEPS, 6)), dma((2,)), dma((2,)),
        dma((gy_n,)), dma((gy_n,)), dma((2,)), dma((2,)),
    ]
    outs = pl.pallas_call(
        functools.partial(kernel_body, (gx_n, gy_n, X, Y, Z, NB)),
        out_shape=(field, field, field, field, jax.ShapeDtypeStruct((BMAX, 16 * DB), f32)),
        in_specs=[smem] * 6 + [hbm] * 9,
        out_specs=(any_spec,) * 5,
        scratch_shapes=scratch,
        compiler_params=pltpu.CompilerParams(
            collective_id=0, has_side_effects=True, vmem_limit_bytes=60 * 1024 * 1024
        ),
        name="yee",
    )(mask.T, owner, ieps, dec, drv, res, e, h, jc, pz, mat, line, slots.reshape(1, -1),
      jnp.asarray(vt), jnp.asarray(wt))
    bufs = [VM((3, X, Y, Z), f32)] * 4
    return pl.pallas_call(
        write_body,
        out_shape=tuple(jax.ShapeDtypeStruct(o.shape, o.dtype) for o in outs),
        in_specs=[any_spec] * 5,
        out_specs=(any_spec,) * 5,
        scratch_shapes=bufs + [VM((BMAX, 16 * DB), f32), dma((5, 3)), dma((5, 3))],
        compiler_params=pltpu.CompilerParams(vmem_limit_bytes=60 * 1024 * 1024),
        name="write",
    )(*outs)


def solution(mesh):
    field = P(None, "gx", "gy", None)
    in_specs = (
        field, field, field, field, P("gx", "gy", None), P(), P(), P(), P(),
        P(None, "gy"), P(), P("gx", "gy", None), P(),
    )
    out_specs = (field, field, field, field, P(("gx", "gy"), None))
    body = functools.partial(shards, gx_n=mesh.shape["gx"], gy_n=mesh.shape["gy"])
    return jax.shard_map(body, mesh=mesh, in_specs=in_specs, out_specs=out_specs, check_vma=False)
```
